128 devices in a mesh: ctx: 32 (over z, x_hi, y), head: 4 (over x_lo, core).
Axes of the slice: x: 4 (x_hi: 2, x_lo: 2; x = x_hi * 2 + x_lo), y: 4, z: 4, core: 2. Of those that a mesh axis runs over, the one named last changes fastest.
Arguments:
- queries: bfloat16 [512, 16384], P('ctx', 'head'), may hold values from -18 to 18
- new_keys: bfloat16 [512, 1024], P('ctx', 'head'), may hold values from -7 to 7
- new_values: bfloat16 [512, 1024], P('ctx', 'head'), may hold values from -6 to 6
- cache_keys: bfloat16 [32768, 1024], P('ctx', 'head'), may hold values from -6 to 6
- cache_values: bfloat16 [32768, 1024], P('ctx', 'head'), may hold values from -6 to 6
- span_ids: int32 [256], P('ctx'), may hold values from 0 to 255, each once
- valid_len: int32 [256], P('ctx'), may hold values from 1 to 128, 20480 in all
- pos_ids: int32 [512], replicated, may hold values from 0 to 511, each once
- offset: int32 [1], replicated, may hold values from 16384 to 32768
- out_weight: bfloat16 [16384, 16384], P('head', 'ctx'), may hold values from -0.046875 to 0.046875
Outputs:
- layer_out: bfloat16 [512, 16384], P('head', 'ctx')
The draws below stay inside these ranges and needn't reach their ends.
Inputs may be any that keep to these rules, and one draw needn't show every extreme that they name: `span_ids`: each span number appears once. `pos_ids`: each position of the turn appears once.
All inputs are finite; a program needn't handle non-finite values. No bound on the sum of `valid_len` on one device may be relied on, other than what follows from the above.
Results may differ from the reference program's by a relative error of at most 0.014.
Values may be sent and summed in bfloat16 or wider, within the bound.
No kernel may reach another device: no remote copies, remote signals or barrier semaphores. Data moves between devices by JAX's collectives and lax.ppermute only.
A program may use at most 128 MiB of HBM per device.

```python
import math
import jax
import jax.numpy as jnp
import numpy as np
from jax import lax

D = 16384
HQ = 128
KVH = 8
HD = 128
SPAN = 128
NEW = 512
CACHE = 32768
SPANS = 256


def draw_queries(key, part):
    key = jax.random.fold_in(key, 11)
    return jnp.clip(3.0 * jax.random.normal(jax.random.fold_in(key, 1), (NEW, HQ * HD), jnp.float32), -18.0, 18.0).astype(jnp.bfloat16)


def draw_cache_keys(key, part):
    key = jax.random.fold_in(key, 23)
    return jnp.clip(jax.random.normal(jax.random.fold_in(key, 1), (CACHE, KVH * HD), jnp.float32), -6.0, 6.0).astype(jnp.bfloat16)


def steps_of(own_key, shape, cuts, smallest, top_value):
    loudness, own = 1.0, jax.random.fold_in(own_key, 6)
    for dim, blocks in cuts:
        heights = jnp.exp(jax.random.uniform(jax.random.fold_in(own, dim), (blocks,), jnp.float32, smallest / len(cuts), top_value / len(cuts)))
        loudness = loudness * jnp.repeat(heights, shape[dim] // blocks).reshape([-1 if axis == dim else 1 for axis in range(len(shape))])
    return loudness


def profile(count, total, limit, slope):
    weights = [(1 << 20) // math.isqrt(grade ** slope) + 1 for grade in range(2, count + 1)]
    surplus, given = total - limit - (count - 1), [1] * (count - 1)
    while surplus > 0:
        movable = [i for i in range(count - 1) if given[i] < limit]
        mass, left = sum([weights[i] for i in movable]), surplus
        for i in movable:
            extra = min(limit - given[i], max(1, left * weights[i] // mass), surplus)
            given[i] = given[i] + extra
            surplus = surplus - extra
    return np.array([limit] + given)


def ragged_sizes(own_key, amount, total, limit, lean):
    if amount == 2:
        one = jax.random.randint(own_key, (), max(1, total - limit), min(limit, total - 1) + 1)
        return jnp.stack([one, total - one])
    tallies = jnp.asarray(profile(amount, total, limit, lean), jnp.int32)
    couples = (amount - 1) // 2
    source_of, sink = tallies[1:1 + 2 * couples:2], tallies[2:2 + 2 * couples:2]
    margin = jnp.minimum(source_of - 1, limit - sink)
    moved = jax.random.randint(jax.random.fold_in(own_key, 1), (couples,), 0, 1 << 20) % (margin + 1)
    tallies = tallies.at[1:1 + 2 * couples:2].set(source_of - moved).at[2:2 + 2 * couples:2].set(sink + moved)
    return tallies[jax.random.permutation(jax.random.fold_in(own_key, 2), amount)]


def scatter_about(stream_key, extent, spread, most, split=(), held_as=jnp.bfloat16):
    result = spread * jax.random.normal(stream_key, extent, jnp.float32)
    if split:
        result = result * steps_of(stream_key, extent, split, -0.22, 0.18)
    return jnp.clip(result, -most, most).astype(held_as)


def setup_inputs(seed: int = 0) -> dict:
    keys = jax.random.split(jax.random.key(seed), 11)
    return {
        "queries": draw_queries(jax.random.fold_in(keys[10], 71), 0),
        "new_keys": scatter_about(keys[1], (NEW, KVH * HD), 1.25, 7.0, ((0, 32), (1, 4))),
        "new_values": scatter_about(keys[2], (NEW, KVH * HD), 1.0, 6.0, ((0, 32), (1, 4))),
        "cache_keys": draw_cache_keys(jax.random.fold_in(keys[10], 71), 0),
        "cache_values": scatter_about(keys[4], (CACHE, KVH * HD), 1.0, 6.0, ((0, 32), (1, 4))),
        "span_ids": jax.random.permutation(keys[5], SPANS).astype(jnp.int32),
        "valid_len": ragged_sizes(keys[6], SPANS, SPANS * SPAN * 5 // 8, SPAN, 1).astype(jnp.int32),
        "pos_ids": jax.random.permutation(keys[7], NEW).astype(jnp.int32),
        "offset": jax.random.randint(keys[8], (1,), CACHE // 2, CACHE + 1).astype(jnp.int32),
        "out_weight": scatter_about(keys[9], (HQ * HD, D), (HQ * HD) ** -0.5, 0.046875, ((0, 4), (1, 32))),
    }


def reference(queries, new_keys, new_values, cache_keys, cache_values, span_ids, valid_len, pos_ids, offset, out_weight):
    group_size = HQ // KVH
    row_index = jnp.arange(CACHE, dtype=jnp.int32)
    slot_index = row_index // SPAN
    within = row_index % SPAN
    cache_position = span_ids[slot_index] * SPAN + within
    cache_visible = (within < valid_len[slot_index]) & (cache_position < offset[0])
    turn_visible = pos_ids[None, :] <= pos_ids[:, None]
    visible = jnp.concatenate([jnp.broadcast_to(cache_visible[None, :], (NEW, CACHE)), turn_visible], axis=1)
    all_keys = jnp.concatenate([cache_keys, new_keys], axis=0)
    all_values = jnp.concatenate([cache_values, new_values], axis=0)
    score_scale = 1.0 / math.sqrt(HD)

    def one_head(head_index):
        kv_index = head_index // group_size
        query_rows = lax.dynamic_slice_in_dim(queries, head_index * HD, HD, 1).astype(jnp.float32)
        key_rows = lax.dynamic_slice_in_dim(all_keys, kv_index * HD, HD, 1).astype(jnp.float32)
        value_rows = lax.dynamic_slice_in_dim(all_values, kv_index * HD, HD, 1).astype(jnp.float32)
        scores = jnp.dot(query_rows, key_rows.T, preferred_element_type=jnp.float32) * score_scale
        scores = jnp.where(visible, scores, -1e+30)
        rowmax = lax.optimization_barrier(jnp.max(scores, axis=1, keepdims=True))
        raw_weights = jnp.where(visible, jnp.exp(scores - rowmax), 0.0)
        totals = lax.optimization_barrier(jnp.sum(raw_weights, axis=1, keepdims=True))
        probabilities = lax.optimization_barrier(raw_weights.astype(jnp.bfloat16)).astype(jnp.float32)
        return jnp.dot(probabilities, value_rows, preferred_element_type=jnp.float32) / totals
    attended = lax.map(one_head, jnp.arange(HQ, dtype=jnp.int32))
    attended = jnp.transpose(attended, (1, 0, 2)).reshape(NEW, HQ * HD).astype(jnp.bfloat16)
    attended = lax.optimization_barrier(attended).astype(jnp.float32)
    layer_out = jnp.dot(attended, out_weight.astype(jnp.float32), preferred_element_type=jnp.float32)
    return layer_out.astype(jnp.bfloat16)
```

```python
import math

import jax
import jax.numpy as jnp
import numpy as np
from jax import lax
from jax.experimental import pallas as pl
from jax.experimental.pallas import tpu as pltpu
from jax.sharding import Mesh
from jax.sharding import PartitionSpec as P

HD = 128
SPAN = 128
KEY_BLOCK = 512
FILL = -1e30
LOG2_SCALE = math.log2(math.e) / math.sqrt(HD)
F32 = jnp.float32
BF16 = jnp.bfloat16
VMEM = pl.BlockSpec(memory_space=pltpu.VMEM)
SMEM = pl.BlockSpec(memory_space=pltpu.SMEM)


def dot_nt(a, b):
    return lax.dot_general(a, b, (((1,), (1,)), ((), ())), preferred_element_type=F32)


def grant(mib):
    return pltpu.CompilerParams(vmem_limit_bytes=mib << 20)


def pack_kernel(place, live, keys, values, new_keys, new_values, *outs):
    slots = live.shape[0]
    rows = slots * SPAN
    fresh = new_keys.shape[0]
    row_id = lax.broadcasted_iota(jnp.int32, (SPAN, HD), 0)
    lane_id = lax.broadcasted_iota(jnp.int32, (16, HD), 1)
    counts = jnp.zeros((16, HD), F32)
    for s in range(slots):
        counts = jnp.where(lane_id == s, live[s].astype(F32), counts)
    for k, out in enumerate(outs):
        head = lax.rem(place[0] + k, 4) // 2
        cols = pl.ds(pl.multiple_of(head * HD, HD), HD)
        for s in range(slots):
            part = pl.ds(s * SPAN, SPAN)
            visible = row_id < live[s]
            key = keys[part, cols].astype(F32)
            key = jnp.where(visible, key, jnp.broadcast_to(key[:1], key.shape))
            out[0, part, :] = key.astype(BF16)
            out[1, part, :] = jnp.where(visible, values[part, cols].astype(F32), 0.0).astype(BF16)
        out[0, rows : rows + fresh, :] = new_keys[:, cols]
        out[1, rows : rows + fresh, :] = new_values[:, cols]
        out[0, rows + fresh :, :] = counts.astype(BF16)
        out[1, rows + fresh :, :] = counts.astype(BF16)


def attend_kernel(live, queries, kv0, kv1, kv2, kv3, pos_q, pos_n, out, kc, vc, kn, vn, scores, fresh_scores, peak, top, acc):
    sources = (kv0, kv1, kv2, kv3)
    slots = live.shape[0] // len(sources)
    rows = slots * SPAN
    fresh = pos_n.shape[1] // len(sources) // 2
    heads = queries.shape[1] // HD
    tokens = queries.shape[0]
    row_id = lax.broadcasted_iota(jnp.int32, (SPAN, HD), 0)

    kn[...] = jnp.zeros_like(kn)
    vn[:, :HD] = jnp.zeros((vn.shape[0], HD), BF16)
    vn[:, HD:] = jnp.ones((vn.shape[0], HD), BF16)
    place = jnp.int32(0)
    for i, kv in enumerate(sources):
        kn[i * fresh : (i + 1) * fresh, :] = kv[0, rows : rows + fresh, :]
        vn[i * fresh : (i + 1) * fresh, :HD] = kv[1, rows : rows + fresh, :]

        def gather_slot(s, at, kv=kv, i=i):
            count = live[i * slots + s]
            source = pl.ds(pl.multiple_of(s * SPAN, SPAN), SPAN)
            target = pl.ds(pl.multiple_of(at, 16), SPAN)
            kc[target, :] = kv[0, source, :]
            vc[target, :HD] = kv[1, source, :]
            vc[target, HD:] = jnp.where(row_id < count, 1.0, 0.0).astype(BF16)
            return at + ((count + 15) // 16) * 16

        place = lax.fori_loop(0, slots, gather_slot, place)
    tail = pl.ds(pl.multiple_of(place, 16), KEY_BLOCK)
    spare = kc[:16, :].astype(F32)[:1]
    kc[tail, :] = jnp.broadcast_to(spare, (KEY_BLOCK, HD)).astype(BF16)
    vc[tail, :] = jnp.zeros((KEY_BLOCK, 2 * HD), BF16)
    blocks = (place + KEY_BLOCK - 1) // KEY_BLOCK

    seen = pos_n[...] <= pos_q[...]
    lane_id = lax.broadcasted_iota(jnp.int32, (tokens, HD), 1)

    def head_cols(h):
        if isinstance(h, int):
            return pl.ds(h * HD, HD)
        return pl.ds(pl.multiple_of(h * HD, HD), HD)

    def block_rows(b):
        return pl.ds(pl.multiple_of(b * KEY_BLOCK, KEY_BLOCK), KEY_BLOCK)

    def score_fresh(h, slot):
        s = jnp.where(seen, dot_nt(queries[:, head_cols(h)], kn[...]), FILL)
        fresh_scores[slot] = s
        peak[...] = s

    def score_block(h, slot, b):
        s = dot_nt(queries[:, head_cols(h)], kc[block_rows(b), :])
        scores[slot, b] = s
        high = peak[...]
        for j in range(KEY_BLOCK // HD):
            high = jnp.maximum(high, s[:, j * HD : (j + 1) * HD])
        peak[...] = high

    def score_end(slot):
        m = jnp.max(peak[...], axis=1, keepdims=True) * LOG2_SCALE
        top[slot] = jnp.broadcast_to(m.astype(BF16).astype(F32), (tokens, HD))

    def weigh_fresh(slot):
        p = jnp.where(seen, jnp.exp2(fresh_scores[slot] * LOG2_SCALE - top[slot]), 0.0)
        acc[...] = jnp.dot(p.astype(BF16), vn[...], preferred_element_type=F32)

    def weigh_block(slot, b):
        m = top[slot]
        p = [
            jnp.exp2(scores[slot, b, :, j * HD : (j + 1) * HD] * LOG2_SCALE - m).astype(BF16)
            for j in range(KEY_BLOCK // HD)
        ]
        p = jnp.concatenate(p, axis=1)
        acc[...] += jnp.dot(p, vc[block_rows(b), :], preferred_element_type=F32)

    def weigh_end(h, slot):
        total = acc[:, HD:]
        high = total.astype(BF16).astype(F32)
        out[:, head_cols(h)] = acc[:, :HD].astype(BF16)
        notes = out[:, heads * HD :].astype(F32)
        notes = jnp.where(lane_id == h, top[slot], notes)
        notes = jnp.where(lane_id == heads + h, high, notes)
        notes = jnp.where(lane_id == 2 * heads + h, total - high, notes)
        out[:, heads * HD :] = notes.astype(BF16)

    out[:, heads * HD :] = jnp.zeros((tokens, HD), BF16)
    score_fresh(0, 0)

    def first(b, _):
        score_block(0, 0, b)
        return _

    lax.fori_loop(0, blocks, first, 0)
    score_end(0)

    def step(h, _):
        slot = lax.rem(h, 2)
        weigh_fresh(1 - slot)
        score_fresh(h, slot)

        def both(b, _):
            weigh_block(1 - slot, b)
            score_block(h, slot, b)
            return _

        lax.fori_loop(0, blocks, both, 0)
        score_end(slot)
        weigh_end(h - 1, 1 - slot)
        return _

    lax.fori_loop(1, heads, step, 0)
    last = (heads - 1) % 2
    weigh_fresh(last)

    def final(b, _):
        weigh_block(last, b)
        return _

    lax.fori_loop(0, blocks, final, 0)
    weigh_end(heads - 1, last)


def settle_kernel(parts, out):
    groups, tokens, width = parts.shape
    heads = width // HD - 1
    notes = [parts[g, :, heads * HD :].astype(F32) for g in range(groups)]
    highest = notes[0]
    for g in range(1, groups):
        highest = jnp.maximum(highest, notes[g])
    factors = [jnp.exp2(notes[g] - highest) for g in range(groups)]
    for h in range(heads):
        cols = slice(h * HD, (h + 1) * HD)
        numerator = jnp.zeros((tokens, HD), F32)
        total = jnp.zeros((tokens, 1), F32)
        for g in range(groups):
            factor = factors[g][:, h : h + 1]
            numerator += factor * parts[g, :, cols].astype(F32)
            total += factor * (
                notes[g][:, heads + h : heads + h + 1] + notes[g][:, 2 * heads + h : 2 * heads + h + 1]
            )
        attended = (numerator / total).astype(BF16)
        for g in range(groups):
            out[g, :, cols] = attended


def project_kernel(place, attended, w0, w1, w2, w3, out):
    for k, w in enumerate((w0, w1, w2, w3)):
        target = lax.rem(place[0] + 4 - k, 4)
        for r in range(out.shape[1]):
            rows = slice(r * out.shape[2], (r + 1) * out.shape[2])
            out[target, r] = jnp.dot(attended[rows, :], w[...], preferred_element_type=F32).astype(BF16)


def swap(x, axes):
    return lax.all_to_all(x, axes, split_axis=0, concat_axis=0, tiled=False)


def along_y(x, distance):
    return lax.ppermute(x, "y", [(i, (i + distance) % 4) for i in range(4)])


def shards(
    queries,
    new_keys,
    new_values,
    cache_keys,
    cache_values,
    span_ids,
    valid_len,
    pos_ids,
    offset,
    out_weight,
):
    y = lax.axis_index("y")
    group = lax.axis_index("z") * 2 + lax.axis_index("x_hi")
    place = y[None].astype(jnp.int32)
    groups = 8
    fresh, width = queries.shape
    slots = span_ids.shape[0]
    rows = slots * SPAN
    quarter = width // 4
    tokens = pos_ids.shape[0]

    live = jnp.clip(jnp.minimum(valid_len, offset[0] - span_ids * SPAN), 0, SPAN)
    packet = jax.ShapeDtypeStruct((2, rows + fresh + 16, HD), BF16)
    with jax.named_scope("pack"):
        packets = pl.pallas_call(
            pack_kernel,
            out_shape=[packet] * 4,
            in_specs=[SMEM, SMEM] + [VMEM] * 4,
            out_specs=[VMEM] * 4,
            compiler_params=grant(24),
            cost_estimate=pl.CostEstimate(flops=0, bytes_accessed=4 << 20, transcendentals=0),
        )(place, live, cache_keys, cache_values, new_keys, new_values)
    with jax.named_scope("move_kv"):
        kv = [packets[0]] + [along_y(packets[k], k) for k in range(1, 4)]

    with jax.named_scope("move_queries"):
        mine = swap(queries.reshape(fresh, 4, quarter).transpose(1, 0, 2), "y")
        mine = mine.reshape(4 * fresh, quarter)
        mine = swap(jnp.broadcast_to(mine[None], (groups,) + mine.shape), ("z", "x_hi"))
        mine = mine.reshape(tokens, quarter)

    lives = [live] + [kv[k][0, rows + fresh, :slots].astype(jnp.int32) for k in range(1, 4)]
    pos_n = [
        lax.dynamic_slice_in_dim(pos_ids, (group * 4 + lax.rem(y + 4 - k, 4)) * fresh, fresh) for k in range(4)
    ]
    pos_n = jnp.concatenate(pos_n + [jnp.full((4 * fresh,), 1 << 30, jnp.int32)])[None]
    pos_q = pos_ids[:, None]
    all_live = jnp.concatenate(lives)

    with jax.named_scope("move_weight"):
        late = jnp.minimum(sum(l[0] for l in lives), 0)
        weights = [lax.dynamic_slice_in_dim(out_weight, y * quarter, quarter)]
        for k in range(1, 4):
            first = lax.rem(y + k, 4) * quarter + late
            weights.append(along_y(lax.dynamic_slice_in_dim(out_weight, first, quarter), k))

    capacity = 4 * rows + KEY_BLOCK
    most_blocks = -(-4 * rows // KEY_BLOCK)
    heads = quarter // HD
    with jax.named_scope("attend"):
        partial = pl.pallas_call(
            attend_kernel,
            out_shape=jax.ShapeDtypeStruct((tokens, quarter + HD), BF16),
            in_specs=[SMEM] + [VMEM] * 7,
            out_specs=VMEM,
            scratch_shapes=[
                pltpu.VMEM((capacity, HD), BF16),
                pltpu.VMEM((capacity, 2 * HD), BF16),
                pltpu.VMEM((8 * fresh, HD), BF16),
                pltpu.VMEM((8 * fresh, 2 * HD), BF16),
                pltpu.VMEM((2, most_blocks, tokens, KEY_BLOCK), F32),
                pltpu.VMEM((2, tokens, HD), F32),
                pltpu.VMEM((tokens, HD), F32),
                pltpu.VMEM((2, tokens, HD), F32),
                pltpu.VMEM((tokens, 2 * HD), F32),
            ],
            compiler_params=grant(40),
            cost_estimate=pl.CostEstimate(
                flops=8 * tokens * quarter * rows, bytes_accessed=5 << 20, transcendentals=tokens * heads * rows * 2
            ),
        )(all_live, mine, *kv, pos_q, pos_n)

    with jax.named_scope("move_partials"):
        partial = swap(partial.reshape(groups, tokens // groups, quarter + HD), ("z", "x_hi"))
    with jax.named_scope("settle"):
        attended = pl.pallas_call(
            settle_kernel,
            out_shape=jax.ShapeDtypeStruct((groups, tokens // groups, quarter), BF16),
            in_specs=[VMEM],
            out_specs=VMEM,
            compiler_params=grant(24),
            cost_estimate=pl.CostEstimate(flops=1 << 22, bytes_accessed=2 << 20, transcendentals=0),
        )(partial)
    with jax.named_scope("move_attended"):
        attended = swap(attended, ("z", "x_hi")).reshape(tokens, quarter)

    with jax.named_scope("project"):
        columns = out_weight.shape[1]
        terms = pl.pallas_call(
            project_kernel,
            out_shape=jax.ShapeDtypeStruct((4, 4, tokens // 4, columns), BF16),
            in_specs=[SMEM] + [VMEM] * 5,
            out_specs=VMEM,
            compiler_params=grant(32),
            cost_estimate=pl.CostEstimate(
                flops=8 * tokens * quarter * columns, bytes_accessed=7 << 20, transcendentals=0
            ),
        )(place, attended, *weights)
    with jax.named_scope("move_terms"):
        terms = swap(terms.reshape(16, tokens // 4, columns), ("y", "x_lo", "core"))
    return jnp.sum(terms.astype(F32), axis=0).astype(BF16)


def solution(mesh):
    fine = Mesh(mesh.devices.reshape(4, 2, 4, 2, 2), ("z", "x_hi", "y", "x_lo", "core"))
    ctx, head = ("z", "x_hi", "y"), ("x_lo", "core")
    in_specs = (
        P(ctx, head),
        P(ctx, head),
        P(ctx, head),
        P(ctx, head),
        P(ctx, head),
        P(ctx),
        P(ctx),
        P(),
        P(),
        P(head, ctx),
    )
    return jax.shard_map(shards, mesh=fine, in_specs=in_specs, out_specs=P(head, ctx), check_vma=False)
```

```python
import math

import jax
import jax.numpy as jnp
import numpy as np
from jax import lax
from jax.experimental import pallas as pl
from jax.experimental.pallas import tpu as pltpu
from jax.sharding import Mesh
from jax.sharding import PartitionSpec as P

HD = 128
SPAN = 128
KEY_BLOCK = 512
FILL = -1e30
LOG2_SCALE = math.log2(math.e) / math.sqrt(HD)
F32 = jnp.float32
BF16 = jnp.bfloat16
TINY = pl.CostEstimate(flops=1, bytes_accessed=1, transcendentals=0)
VMEM = pl.BlockSpec(memory_space=pltpu.VMEM)
SMEM = pl.BlockSpec(memory_space=pltpu.SMEM)


def dot_nt(a, b):
    return lax.dot_general(a, b, (((1,), (1,)), ((), ())), preferred_element_type=F32)


def grant(mib):
    return pltpu.CompilerParams(vmem_limit_bytes=mib << 20)


def pack_kernel(place, live, keys, values, new_keys, new_values, *outs):
    slots = live.shape[0]
    rows = slots * SPAN
    fresh = new_keys.shape[0]
    row_id = lax.broadcasted_iota(jnp.int32, (SPAN, HD), 0)
    lane_id = lax.broadcasted_iota(jnp.int32, (16, HD), 1)
    counts = jnp.zeros((16, HD), F32)
    for s in range(slots):
        counts = jnp.where(lane_id == s, live[s].astype(F32), counts)
    for k, out in enumerate(outs):
        head = lax.rem(place[0] + k, 2)
        cols = pl.ds(pl.multiple_of(head * HD, HD), HD)
        for s in range(slots):
            part = pl.ds(s * SPAN, SPAN)
            visible = row_id < live[s]
            key = keys[part, cols].astype(F32)
            key = jnp.where(visible, key, jnp.broadcast_to(key[:1], key.shape))
            out[0, part, :] = key.astype(BF16)
            out[1, part, :] = jnp.where(visible, values[part, cols].astype(F32), 0.0).astype(BF16)
        out[0, rows : rows + fresh, :] = new_keys[:, cols]
        out[1, rows : rows + fresh, :] = new_values[:, cols]
        out[0, rows + fresh :, :] = counts.astype(BF16)
        out[1, rows + fresh :, :] = counts.astype(BF16)


def attend_kernel(live, here, queries, *refs):
    near, far = refs[:4], refs[4:8]
    pos_q, pos_n, out, kc, vc, kn, vn, scores, fresh_scores, peak, top, acc = refs[8:]
    slots = live.shape[0] // len(near)
    rows = slots * SPAN
    fresh = pos_n.shape[1] // len(near) // 2
    heads = queries.shape[1] // HD
    tokens = queries.shape[0]
    row_id = lax.broadcasted_iota(jnp.int32, (SPAN, HD), 0)

    kn[...] = jnp.zeros_like(kn)
    vn[:, :HD] = jnp.zeros((vn.shape[0], HD), BF16)
    vn[:, HD:] = jnp.ones((vn.shape[0], HD), BF16)
    def collect(sources):
        place = jnp.int32(0)
        for i, kv in enumerate(sources):
            kn[i * fresh : (i + 1) * fresh, :] = kv[0, rows : rows + fresh, :]
            vn[i * fresh : (i + 1) * fresh, :HD] = kv[1, rows : rows + fresh, :]

            def gather_slot(s, at, kv=kv, i=i):
                count = live[i * slots + s]
                source = pl.ds(pl.multiple_of(s * SPAN, SPAN), SPAN)
                target = pl.ds(pl.multiple_of(at, 16), SPAN)
                kc[target, :] = kv[0, source, :]
                vc[target, :HD] = kv[1, source, :]
                vc[target, HD:] = jnp.where(row_id < count, 1.0, 0.0).astype(BF16)
                return at + ((count + 15) // 16) * 16

            place = lax.fori_loop(0, slots, gather_slot, place)

    @pl.when(here[0] == 1)
    def _():
        collect(near)

    @pl.when(here[0] != 1)
    def _():
        collect(far)

    place = lax.fori_loop(0, live.shape[0], lambda s, at: at + ((live[s] + 15) // 16) * 16, jnp.int32(0))
    tail = pl.ds(pl.multiple_of(place, 16), KEY_BLOCK)
    spare = kc[:16, :].astype(F32)[:1]
    kc[tail, :] = jnp.broadcast_to(spare, (KEY_BLOCK, HD)).astype(BF16)
    vc[tail, :] = jnp.zeros((KEY_BLOCK, 2 * HD), BF16)
    blocks = (place + KEY_BLOCK - 1) // KEY_BLOCK

    seen = pos_n[...] <= pos_q[...]
    lane_id = lax.broadcasted_iota(jnp.int32, (tokens, HD), 1)

    def head_cols(h):
        if isinstance(h, int):
            return pl.ds(h * HD, HD)
        return pl.ds(pl.multiple_of(h * HD, HD), HD)

    def block_rows(b):
        return pl.ds(pl.multiple_of(b * KEY_BLOCK, KEY_BLOCK), KEY_BLOCK)

    def score_fresh(h, slot):
        s = jnp.where(seen, dot_nt(queries[:, head_cols(h)], kn[...]), FILL)
        fresh_scores[slot] = s
        peak[...] = s

    def score_block(h, slot, b):
        s = dot_nt(queries[:, head_cols(h)], kc[block_rows(b), :])
        scores[slot, b] = s
        high = peak[...]
        for j in range(KEY_BLOCK // HD):
            high = jnp.maximum(high, s[:, j * HD : (j + 1) * HD])
        peak[...] = high

    def score_end(slot):
        m = jnp.max(peak[...], axis=1, keepdims=True) * LOG2_SCALE
        top[slot] = jnp.broadcast_to(m.astype(BF16).astype(F32), (tokens, HD))

    def weigh_fresh(slot):
        p = jnp.where(seen, jnp.exp2(fresh_scores[slot] * LOG2_SCALE - top[slot]), 0.0)
        acc[...] = jnp.dot(p.astype(BF16), vn[...], preferred_element_type=F32)

    def weigh_block(slot, b):
        m = top[slot]
        p = [
            jnp.exp2(scores[slot, b, :, j * HD : (j + 1) * HD] * LOG2_SCALE - m).astype(BF16)
            for j in range(KEY_BLOCK // HD)
        ]
        p = jnp.concatenate(p, axis=1)
        acc[...] += jnp.dot(p, vc[block_rows(b), :], preferred_element_type=F32)

    def weigh_end(h, slot):
        total = acc[:, HD:]
        high = total.astype(BF16).astype(F32)
        out[:, head_cols(h)] = acc[:, :HD].astype(BF16)
        notes = out[:, heads * HD :].astype(F32)
        notes = jnp.where(lane_id == h, top[slot], notes)
        notes = jnp.where(lane_id == heads + h, high, notes)
        notes = jnp.where(lane_id == 2 * heads + h, total - high, notes)
        out[:, heads * HD :] = notes.astype(BF16)

    out[:, heads * HD :] = jnp.zeros((tokens, HD), BF16)
    score_fresh(0, 0)

    def first(b, _):
        score_block(0, 0, b)
        return _

    lax.fori_loop(0, blocks, first, 0)
    score_end(0)

    def step(h, _):
        slot = lax.rem(h, 2)
        weigh_fresh(1 - slot)
        score_fresh(h, slot)

        def both(b, _):
            weigh_block(1 - slot, b)
            score_block(h, slot, b)
            return _

        lax.fori_loop(0, blocks, both, 0)
        score_end(slot)
        weigh_end(h - 1, 1 - slot)
        return _

    lax.fori_loop(1, heads, step, 0)
    last = (heads - 1) % 2
    weigh_fresh(last)

    def final(b, _):
        weigh_block(last, b)
        return _

    lax.fori_loop(0, blocks, final, 0)
    weigh_end(heads - 1, last)


def settle_kernel(parts, out):
    groups, tokens, width = parts.shape
    heads = width // HD - 1
    notes = [parts[g, :, heads * HD :].astype(F32) for g in range(groups)]
    highest = notes[0]
    for g in range(1, groups):
        highest = jnp.maximum(highest, notes[g])
    factors = [jnp.exp2(notes[g] - highest) for g in range(groups)]
    for h in range(heads):
        cols = slice(h * HD, (h + 1) * HD)
        numerator = jnp.zeros((tokens, HD), F32)
        total = jnp.zeros((tokens, 1), F32)
        for g in range(groups):
            factor = factors[g][:, h : h + 1]
            numerator += factor * parts[g, :, cols].astype(F32)
            total += factor * (
                notes[g][:, heads + h : heads + h + 1] + notes[g][:, 2 * heads + h : 2 * heads + h + 1]
            )
        attended = (numerator / total).astype(BF16)
        for g in range(groups):
            out[g, :, cols] = attended


def project_kernel(place, attended, w0, w1, w2, w3, out):
    size = out.shape[2]
    picked = [pl.ds(pl.multiple_of((2 * r + place[1]) * size, size), size) for r in range(out.shape[1])]
    rows = jnp.concatenate([attended[p, :] for p in picked], axis=0)
    for k, w in enumerate((w0, w1, w2, w3)):
        target = lax.rem(place[0] + 4 - k, 4)
        term = jnp.dot(rows, w[...], preferred_element_type=F32).astype(BF16)
        for r in range(out.shape[1]):
            out[target, r] = term[r * size : (r + 1) * size]


def swap(x, axes):
    return lax.all_to_all(x, axes, split_axis=0, concat_axis=0, tiled=False)


def along_y(x, distance):
    return lax.ppermute(x, "y", [(i, (i + distance) % 4) for i in range(4)])


def to_other_core(x):
    return lax.ppermute(x, "core", [(0, 1), (1, 0)])


def to_chip(x, distance):
    targets = [((i + distance) % 4) for i in range(4)]
    return lax.ppermute(x, ("y", "core"), [(i * 2 + t // 2, t * 2 + t // 2) for i, t in enumerate(targets)])


def to_sibling(x):
    return lax.ppermute(x, ("y", "core"), [(t * 2 + t // 2, t * 2 + 1 - t // 2) for t in range(4)])


def shards(
    queries,
    new_keys,
    new_values,
    cache_keys,
    cache_values,
    span_ids,
    valid_len,
    pos_ids,
    offset,
    out_weight,
):
    y, core = lax.axis_index("y"), lax.axis_index("core")
    group = lax.axis_index("z") * 2 + lax.axis_index("x_hi")
    place = y[None].astype(jnp.int32)
    here = (y // 2 == core).astype(jnp.int32)[None]
    groups = 8
    fresh, width = queries.shape
    slots = span_ids.shape[0]
    rows = slots * SPAN
    quarter = width // 4
    tokens = pos_ids.shape[0]

    def on_core(mine, other):
        return jnp.where(core == 0, jnp.stack([mine, other]), jnp.stack([other, mine]))

    with jax.named_scope("move_queries"):
        halves = queries.reshape(fresh, 2, 2, quarter).transpose(2, 1, 0, 3)
        other = to_other_core(lax.dynamic_index_in_dim(halves, 1 - core, 0, False))
        mine = on_core(lax.dynamic_index_in_dim(halves, core, 0, False), other)
        mine = jnp.broadcast_to(mine.reshape(1, 4, fresh, quarter), (groups, 4, fresh, quarter))
        mine = swap(mine.reshape(groups * 4, fresh, quarter), ("z", "x_hi", "y")).reshape(tokens, quarter)

    live = jnp.clip(jnp.minimum(valid_len, offset[0] - span_ids * SPAN), 0, SPAN)
    packet = jax.ShapeDtypeStruct((2, rows + fresh + 16, HD), BF16)
    with jax.named_scope("pack"):
        packets = pl.pallas_call(
            pack_kernel,
            out_shape=[packet] * 4,
            in_specs=[SMEM, SMEM] + [VMEM] * 4,
            out_specs=[VMEM] * 4,
            compiler_params=grant(24),
            cost_estimate=TINY,
        )(place, live, cache_keys, cache_values, new_keys, new_values)
    with jax.named_scope("move_kv"):
        near = [packets[0]] + [to_chip(packets[k], k) for k in range(1, 4)]
        near, mine = lax.optimization_barrier((near, mine))
        far = [to_sibling(p) for p in near]

    def counts(k):
        row = jnp.where(here[0] == 1, near[k][0, rows + fresh, :slots], far[k][0, rows + fresh, :slots])
        return row.astype(jnp.int32)

    lives = [counts(k) for k in range(4)]
    pos_n = [
        lax.dynamic_slice_in_dim(pos_ids, (group * 4 + lax.rem(y + 4 - k, 4)) * fresh, fresh) for k in range(4)
    ]
    pos_n = jnp.concatenate(pos_n + [jnp.full((4 * fresh,), 1 << 30, jnp.int32)])[None]
    pos_q = pos_ids[:, None]
    all_live = jnp.concatenate(lives)

    with jax.named_scope("move_weight"):
        halves = out_weight.reshape(2, 2, quarter, out_weight.shape[1])
        other = to_other_core(lax.dynamic_index_in_dim(halves, 1 - core, 1, False))

        def chunk(k):
            chip = lax.rem(y + k, 4)
            own = lax.dynamic_slice(halves, (chip % 2, core, 0, 0), (1, 1) + halves.shape[2:])[0, 0]
            return jnp.where(chip // 2 == core, own, lax.dynamic_index_in_dim(other, chip % 2, 0, False))

        chunks = [chunk(k) for k in range(4)]
        late, _ = lax.optimization_barrier((chunks[1:], near[1:]))
        weights = [chunks[0]] + [along_y(late[k - 1], k) for k in range(1, 4)]
        mine, _ = lax.optimization_barrier((mine, late))

    capacity = 4 * rows + KEY_BLOCK
    most_blocks = -(-4 * rows // KEY_BLOCK)
    heads = quarter // HD
    with jax.named_scope("attend"):
        partial = pl.pallas_call(
            attend_kernel,
            out_shape=jax.ShapeDtypeStruct((tokens, quarter + HD), BF16),
            in_specs=[SMEM, SMEM] + [VMEM] * 11,
            out_specs=VMEM,
            scratch_shapes=[
                pltpu.VMEM((capacity, HD), BF16),
                pltpu.VMEM((capacity, 2 * HD), BF16),
                pltpu.VMEM((8 * fresh, HD), BF16),
                pltpu.VMEM((8 * fresh, 2 * HD), BF16),
                pltpu.VMEM((2, most_blocks, tokens, KEY_BLOCK), F32),
                pltpu.VMEM((2, tokens, HD), F32),
                pltpu.VMEM((tokens, HD), F32),
                pltpu.VMEM((2, tokens, HD), F32),
                pltpu.VMEM((tokens, 2 * HD), F32),
            ],
            compiler_params=grant(40),
            cost_estimate=TINY,
        )(all_live, here, mine, *near, *far, pos_q, pos_n)

    with jax.named_scope("move_partials"):
        partial = swap(partial.reshape(groups, tokens // groups, quarter + HD), ("z", "x_hi"))
    with jax.named_scope("settle"):
        attended = pl.pallas_call(
            settle_kernel,
            out_shape=jax.ShapeDtypeStruct((groups, tokens // groups, quarter), BF16),
            in_specs=[VMEM],
            out_specs=VMEM,
            compiler_params=grant(24),
            cost_estimate=TINY,
        )(partial)
    with jax.named_scope("move_attended"):
        attended = swap(attended, ("z", "x_hi")).reshape(tokens, quarter)

    columns = out_weight.shape[1]

    def project(which):
        return pl.pallas_call(
            project_kernel,
            out_shape=jax.ShapeDtypeStruct((4, 2, tokens // 4, columns), BF16),
            in_specs=[SMEM] + [VMEM] * 5,
            out_specs=VMEM,
            compiler_params=grant(32),
            cost_estimate=TINY,
        )(jnp.stack([y, which]).astype(jnp.int32), attended, *weights)

    with jax.named_scope("project"):
        theirs = to_other_core(project(1 - core))
        terms = (project(core).astype(F32) + theirs.astype(F32)).astype(BF16)
    with jax.named_scope("move_terms"):
        terms = swap(terms.reshape(8, tokens // 4, columns), ("y", "x_lo"))
    return jnp.sum(terms.astype(F32), axis=0).astype(BF16)


def solution(mesh):
    fine = Mesh(mesh.devices.reshape(4, 2, 4, 2, 2), ("z", "x_hi", "y", "x_lo", "core"))
    ctx, head = ("z", "x_hi", "y"), ("x_lo", "core")
    in_specs = (
        P(ctx, head),
        P(ctx, head),
        P(ctx, head),
        P(ctx, head),
        P(ctx, head),
        P(ctx),
        P(ctx),
        P(),
        P(),
        P(head, ctx),
    )
    return jax.shard_map(shards, mesh=fine, in_specs=in_specs, out_specs=P(head, ctx), check_vma=False)
```

```python
import functools
import math

import jax
import jax.numpy as jnp
import numpy as np
from jax import lax
from jax.experimental import pallas as pl
from jax.experimental.pallas import tpu as pltpu
from jax.sharding import Mesh
from jax.sharding import PartitionSpec as P

HD = 128
SPAN = 128
KEY_BLOCK = 512
FILL = -1e30
LOWEST = -1e20
LOG2_SCALE = math.log2(math.e) / math.sqrt(HD)
F32 = jnp.float32
BF16 = jnp.bfloat16
TINY = pl.CostEstimate(flops=1, bytes_accessed=1, transcendentals=0)
VMEM = pl.BlockSpec(memory_space=pltpu.VMEM)
SMEM = pl.BlockSpec(memory_space=pltpu.SMEM)
ANY = pl.BlockSpec(memory_space=pl.ANY)


def dot_nt(a, b):
    return lax.dot_general(a, b, (((1,), (1,)), ((), ())), preferred_element_type=F32)


def grant(mib):
    return pltpu.CompilerParams(vmem_limit_bytes=mib << 20)


def pack_kernel(place, live, keys_in, values_in, new_keys_in, new_values_in, *refs):
    outs, (keys, values, new_keys, new_values, sems) = refs[:4], refs[4:]
    copies = [
        pltpu.make_async_copy(source, target, sems.at[i])
        for i, (source, target) in enumerate(
            ((keys_in, keys), (values_in, values), (new_keys_in, new_keys), (new_values_in, new_values))
        )
    ]
    for copy in copies:
        copy.start()
    for copy in copies:
        copy.wait()
    slots = live.shape[0]
    rows = slots * SPAN
    fresh = new_keys.shape[0]
    row_id = lax.broadcasted_iota(jnp.int32, (SPAN, HD), 0)
    lane_id = lax.broadcasted_iota(jnp.int32, (16, HD), 1)
    counts = jnp.zeros((16, HD), F32)
    for s in range(slots):
        counts = jnp.where(lane_id == s, live[s].astype(F32), counts)
    for k, out in enumerate(outs):
        head = lax.rem(place[0] + k, 2)
        cols = pl.ds(pl.multiple_of(head * HD, HD), HD)
        for s in range(slots):
            part = pl.ds(s * SPAN, SPAN)
            visible = row_id < live[s]
            key = keys[part, cols].astype(F32)
            key = jnp.where(visible, key, jnp.broadcast_to(key[:1], key.shape))
            out[0, part, :] = key.astype(BF16)
            out[1, part, :] = jnp.where(visible, values[part, cols].astype(F32), 0.0).astype(BF16)
        out[0, rows : rows + fresh, :] = new_keys[:, cols]
        out[1, rows : rows + fresh, :] = new_values[:, cols]
        out[0, rows + fresh :, :] = counts.astype(BF16)
        out[1, rows + fresh :, :] = counts.astype(BF16)


def attend_kernel(live, here, queries, near, far, pos_q, pos_n, out, kc, vc, top, acc):
    slots = live.shape[0] // near.shape[0]
    rows = slots * SPAN
    fresh = near.shape[2] - rows - 16
    heads = queries.shape[1] // HD
    tokens = queries.shape[0]
    row_id = lax.broadcasted_iota(jnp.int32, (SPAN, HD), 0)
    start = near.shape[0] * fresh

    def rounded(count):
        return ((count + 15) // 16) * 16

    def collect(sources):
        place = jnp.int32(start)
        for i in range(sources.shape[0]):
            kv = sources.at[i]
            target = slice(i * fresh, (i + 1) * fresh)
            kc[target, :] = kv[0, rows : rows + fresh, :]
            vc[target, :HD] = kv[1, rows : rows + fresh, :]
            vc[target, HD:] = jnp.ones((fresh, HD), BF16)

            def gather_slot(s, at, kv=kv, i=i):
                count = live[i * slots + s]
                source = pl.ds(pl.multiple_of(s * SPAN, SPAN), SPAN)
                target = pl.ds(pl.multiple_of(at, 16), SPAN)
                kc[target, :] = kv[0, source, :]
                vc[target, :HD] = kv[1, source, :]
                vc[target, HD:] = jnp.where(row_id < count, 1.0, 0.0).astype(BF16)
                return at + rounded(count)

            place = lax.fori_loop(0, slots, gather_slot, place)

    pl.when(here[0] == 1)(functools.partial(collect, near))
    pl.when(here[0] != 1)(functools.partial(collect, far))

    place = lax.fori_loop(0, live.shape[0], lambda s, at: at + rounded(live[s]), jnp.int32(start))
    tail = pl.ds(pl.multiple_of(place, 16), KEY_BLOCK)
    spare = kc[start : start + 16, :].astype(F32)[:1]
    spare = jnp.where(place > start, spare, 0.0)
    kc[tail, :] = jnp.broadcast_to(spare, (KEY_BLOCK, HD)).astype(BF16)
    vc[tail, :] = jnp.zeros((KEY_BLOCK, 2 * HD), BF16)
    blocks = (place + KEY_BLOCK - 1) // KEY_BLOCK

    lane_id = lax.broadcasted_iota(jnp.int32, (tokens, HD), 1)
    key_id = lax.broadcasted_iota(jnp.int32, (1, KEY_BLOCK), 1)
    seen = jnp.where(key_id < place, pos_n[...], tokens) <= pos_q[...]
    lanes = [slice(j * HD, (j + 1) * HD) for j in range(KEY_BLOCK // HD)]

    def head_cols(h):
        return slice(h * HD, (h + 1) * HD)

    def rounded_max(s):
        high = functools.reduce(jnp.maximum, [s[:, g] for g in lanes])
        m = jnp.maximum(jnp.max(high, axis=1, keepdims=True) * LOG2_SCALE, LOWEST)
        return jnp.broadcast_to(m.astype(BF16).astype(F32), (tokens, HD))

    def score(h, part):
        return dot_nt(queries[:, head_cols(h)], kc[part, :])

    def sums(s, m, part):
        p = jnp.concatenate([jnp.exp2(s[:, g] * LOG2_SCALE - m).astype(BF16) for g in lanes], axis=1)
        return jnp.dot(p, vc[part, :], preferred_element_type=F32)

    def begin(h, part, s):
        s = jnp.where(seen, s, FILL)
        m = rounded_max(s)
        top[h] = m
        acc[h] = sums(s, m, part)

    def add(h, part, s):
        old = top[h]
        m = jnp.maximum(old, rounded_max(s))
        top[h] = m
        shrink = jnp.exp2(old - m)
        term = sums(s, m, part)
        acc[h, :, :HD] = acc[h, :, :HD] * shrink + term[:, :HD]
        acc[h, :, HD:] = acc[h, :, HD:] * shrink + term[:, HD:]

    def every_head(visit, part):
        s = score(0, part)
        for h in range(heads):
            following = score(h + 1, part) if h + 1 < heads else None
            visit(h, part, s)
            s = following

    every_head(begin, slice(0, KEY_BLOCK))

    def step(b, _):
        every_head(add, pl.ds(pl.multiple_of(b * KEY_BLOCK, KEY_BLOCK), KEY_BLOCK))
        return _

    lax.fori_loop(1, blocks, step, 0)

    notes = jnp.zeros((tokens, HD), F32)
    for h in range(heads):
        total = acc[h, :, HD:]
        high = total.astype(BF16).astype(F32)
        out[:, head_cols(h)] = acc[h, :, :HD].astype(BF16)
        notes = jnp.where(lane_id == h, top[h], notes)
        notes = jnp.where(lane_id == heads + h, high, notes)
        notes = jnp.where(lane_id == 2 * heads + h, total - high, notes)
    out[:, heads * HD :] = notes.astype(BF16)


def settle_kernel(parts, out):
    groups, tokens, width = parts.shape
    heads = width // HD - 1
    notes = [parts[g, :, heads * HD :].astype(F32) for g in range(groups)]
    highest = notes[0]
    for g in range(1, groups):
        highest = jnp.maximum(highest, notes[g])
    factors = [jnp.exp2(notes[g] - highest) for g in range(groups)]
    for h in range(heads):
        cols = slice(h * HD, (h + 1) * HD)
        numerator = jnp.zeros((tokens, HD), F32)
        total = jnp.zeros((tokens, 1), F32)
        for g in range(groups):
            factor = factors[g][:, h : h + 1]
            numerator += factor * parts[g, :, cols].astype(F32)
            total += factor * (
                notes[g][:, heads + h : heads + h + 1] + notes[g][:, 2 * heads + h : 2 * heads + h + 1]
            )
        attended = (numerator / total).astype(BF16)
        for g in range(groups):
            out[g, :, cols] = attended


def cut_kernel(place, mine, other, *refs):
    outs, held, arrived, left = refs[:8], refs[8], refs[9], refs[10]
    early, late = outs[0].shape[0], outs[1].shape[0]
    pieces = [(i // 2, (i % 2) * early, (early, late)[i % 2]) for i in range(8)]
    pages = [held.at[k, slice(start, start + size), :] for k, start, size in pieces]

    def arrivals(source):
        made = []
        for i, (k, start, size) in enumerate(pieces):
            chip = lax.rem(place[0] + k, 4)
            first = (lax.rem(chip, 2) * 2 + place[1]) * (early + late) + start
            part = pl.ds(pl.multiple_of(first, 16), size)
            made.append((chip // 2 == place[1], pltpu.make_async_copy(source.at[part, :], pages[i], arrived.at[i])))
        return made

    for here, copy in arrivals(mine):
        pl.when(here)(copy.start)
    for here, copy in arrivals(other):
        pl.when(jnp.logical_not(here))(copy.start)
    departures = [pltpu.make_async_copy(pages[i], outs[i], left.at[i]) for i in range(8)]
    for (_, copy), departure in zip(arrivals(mine), departures):
        copy.wait()
        departure.start()
    for departure in departures:
        departure.wait()


def project_kernel(place, attended, *refs):
    out = refs[8]
    size = out.shape[2]
    half = refs[0].shape[0]
    picked = [pl.ds(pl.multiple_of((2 * r + place[1]) * size, size), size) for r in range(out.shape[1])]
    rows = jnp.concatenate([attended[p, :] for p in picked], axis=0)
    for k in range(4):
        target = lax.rem(place[0] + 4 - k, 4)
        term = jnp.dot(rows[:, :half], refs[k][...], preferred_element_type=F32)
        term += jnp.dot(rows[:, half:], refs[4 + k][...], preferred_element_type=F32)
        term = term.astype(BF16)
        for r in range(out.shape[1]):
            out[target, r] = term[r * size : (r + 1) * size]


def swap(x, axes):
    return lax.all_to_all(x, axes, split_axis=0, concat_axis=0, tiled=False)


def along_y(x, distance):
    return lax.ppermute(x, "y", [(i, (i + distance) % 4) for i in range(4)])


def to_other_core(x):
    return lax.ppermute(x, "core", [(0, 1), (1, 0)])


def to_chip(x, distance):
    targets = [((i + distance) % 4) for i in range(4)]
    return lax.ppermute(x, ("y", "core"), [(i * 2 + t // 2, t * 2 + t // 2) for i, t in enumerate(targets)])


def to_sibling(x):
    return lax.ppermute(x, ("y", "core"), [(t * 2 + t // 2, t * 2 + 1 - t // 2) for t in range(4)])


def shards(
    queries,
    new_keys,
    new_values,
    cache_keys,
    cache_values,
    span_ids,
    valid_len,
    pos_ids,
    offset,
    out_weight,
):
    y, core = lax.axis_index("y"), lax.axis_index("core")
    group = lax.axis_index("z") * 2 + lax.axis_index("x_hi")
    place = y[None].astype(jnp.int32)
    here = (y // 2 == core).astype(jnp.int32)[None]
    groups = 8
    fresh, width = queries.shape
    slots = span_ids.shape[0]
    rows = slots * SPAN
    quarter = width // 4
    tokens = pos_ids.shape[0]

    live = jnp.clip(jnp.minimum(valid_len, offset[0] - span_ids * SPAN), 0, SPAN)
    packet = jax.ShapeDtypeStruct((2, rows + fresh + 16, HD), BF16)
    with jax.named_scope("pack"):
        packets = pl.pallas_call(
            pack_kernel,
            out_shape=[packet] * 4,
            in_specs=[SMEM, SMEM] + [ANY] * 4,
            out_specs=[VMEM] * 4,
            scratch_shapes=[
                pltpu.VMEM(cache_keys.shape, BF16),
                pltpu.VMEM(cache_keys.shape, BF16),
                pltpu.VMEM(new_keys.shape, BF16),
                pltpu.VMEM(new_keys.shape, BF16),
                pltpu.SemaphoreType.DMA((4,)),
            ],
            compiler_params=grant(56),
            cost_estimate=TINY,
        )(place, live, cache_keys, cache_values, new_keys, new_values)
    with jax.named_scope("move_queries"):
        halves = queries.reshape(fresh, 2, 2, quarter).transpose(1, 2, 0, 3)
        halves = jnp.broadcast_to(halves[None], (2, 2, 2, fresh, quarter)).reshape(8, fresh, quarter)
        halves = swap(halves, ("y", "core")).reshape(4, 2, fresh, quarter)
        halves, packets = lax.optimization_barrier((halves, packets))
        mine = lax.dynamic_index_in_dim(halves, y // 2, 1, False).reshape(4 * fresh, quarter)
        mine = jnp.broadcast_to(mine[None], (groups,) + mine.shape)
        mine = swap(mine, ("z", "x_hi")).reshape(tokens, quarter)

    with jax.named_scope("move_weight"):
        early = quarter // 2
        chunks = pl.pallas_call(
            cut_kernel,
            out_shape=[
                jax.ShapeDtypeStruct((size, out_weight.shape[1]), BF16) for size in (early, quarter - early) * 4
            ],
            in_specs=[SMEM, ANY, ANY],
            out_specs=[ANY] * 8,
            scratch_shapes=[
                pltpu.VMEM((4, quarter, out_weight.shape[1]), BF16),
                pltpu.SemaphoreType.DMA((8,)),
                pltpu.SemaphoreType.DMA((8,)),
            ],
            compiler_params=grant(56),
            cost_estimate=TINY,
        )(jnp.stack([y, core]).astype(jnp.int32), out_weight, to_other_core(out_weight))
    with jax.named_scope("move_kv"):
        near = [packets[0]] + [to_chip(packets[k], k) for k in range(1, 4)]
    with jax.named_scope("move_weight"):
        late, arrived = lax.optimization_barrier((chunks[2:], near[1:]))
        first = [chunks[0]] + [along_y(late[2 * k - 2], k) for k in range(1, 4)]
        second = [chunks[1]] + [along_y(late[2 * k - 1], k) for k in range(1, 4)]

    with jax.named_scope("move_kv"):
        near = jnp.stack(near)
        near, mine, chunks = lax.optimization_barrier((near, mine, chunks))
        far = to_sibling(near)
        rows_of_counts = jnp.where(here[0] == 1, near[:, 0, rows + fresh, :slots], far[:, 0, rows + fresh, :slots])
        all_live = rows_of_counts.astype(jnp.int32).reshape(-1)

        mine, _ = lax.optimization_barrier((mine, late))

    pos_n = [
        lax.dynamic_slice_in_dim(pos_ids, (group * 4 + lax.rem(y + 4 - k, 4)) * fresh, fresh) for k in range(4)
    ]
    pos_n = jnp.concatenate(pos_n + [jnp.full((KEY_BLOCK - 4 * fresh,), -1, jnp.int32)])[None]
    pos_q = pos_ids[:, None]

    capacity = 4 * (rows + fresh) + KEY_BLOCK
    heads = quarter // HD
    with jax.named_scope("attend"):
        partial = pl.pallas_call(
            attend_kernel,
            out_shape=jax.ShapeDtypeStruct((tokens, quarter + HD), BF16),
            in_specs=[SMEM, SMEM] + [VMEM] * 5,
            out_specs=VMEM,
            scratch_shapes=[
                pltpu.VMEM((capacity, HD), BF16),
                pltpu.VMEM((capacity, 2 * HD), BF16),
                pltpu.VMEM((heads, tokens, HD), F32),
                pltpu.VMEM((heads, tokens, 2 * HD), F32),
            ],
            compiler_params=grant(40),
            cost_estimate=TINY,
        )(all_live, here, mine, near, far, pos_q, pos_n)

    with jax.named_scope("move_partials"):
        partial, first = lax.optimization_barrier((partial, first))
        partial = swap(partial.reshape(groups, tokens // groups, quarter + HD), ("z", "x_hi"))
    with jax.named_scope("settle"):
        attended = pl.pallas_call(
            settle_kernel,
            out_shape=jax.ShapeDtypeStruct((groups, tokens // groups, quarter), BF16),
            in_specs=[VMEM],
            out_specs=VMEM,
            compiler_params=grant(24),
            cost_estimate=TINY,
        )(partial)
    with jax.named_scope("move_attended"):
        attended, second = lax.optimization_barrier((attended, second))
        attended = swap(attended, ("z", "x_hi")).reshape(tokens, quarter)

    columns = out_weight.shape[1]

    def project(which):
        return pl.pallas_call(
            project_kernel,
            out_shape=jax.ShapeDtypeStruct((4, 2, tokens // 4, columns), BF16),
            in_specs=[SMEM] + [VMEM] * 9,
            out_specs=VMEM,
            compiler_params=grant(32),
            cost_estimate=TINY,
        )(jnp.stack([y, which]).astype(jnp.int32), attended, *first, *second)

    with jax.named_scope("project"):
        theirs = to_other_core(project(1 - core))
        terms = (project(core).astype(F32) + theirs.astype(F32)).astype(BF16)
    with jax.named_scope("move_terms"):
        terms = swap(terms.reshape(8, tokens // 4, columns), ("y", "x_lo"))
    return jnp.sum(terms.astype(F32), axis=0).astype(BF16)


def solution(mesh):
    fine = Mesh(mesh.devices.reshape(4, 2, 4, 2, 2), ("z", "x_hi", "y", "x_lo", "core"))
    ctx, head = ("z", "x_hi", "y"), ("x_lo", "core")
    in_specs = (
        P(ctx, head),
        P(ctx, head),
        P(ctx, head),
        P(ctx, head),
        P(ctx, head),
        P(ctx),
        P(ctx),
        P(),
        P(),
        P(head, ctx),
    )
    return jax.shard_map(shards, mesh=fine, in_specs=in_specs, out_specs=P(head, ctx), check_vma=False)
```

```python
import functools
import math

import jax
import jax.numpy as jnp
import numpy as np
from jax import lax
from jax.experimental import pallas as pl
from jax.experimental.pallas import tpu as pltpu
from jax.sharding import Mesh
from jax.sharding import PartitionSpec as P

HD = 128
SPAN = 128
KEY_BLOCK = 512
PIECES = 3
FILL = -1e30
LOWEST = -1e20
LOG2_SCALE = math.log2(math.e) / math.sqrt(HD)
F32 = jnp.float32
BF16 = jnp.bfloat16
TINY = pl.CostEstimate(flops=1, bytes_accessed=1, transcendentals=0)
VMEM = pl.BlockSpec(memory_space=pltpu.VMEM)
SMEM = pl.BlockSpec(memory_space=pltpu.SMEM)
ANY = pl.BlockSpec(memory_space=pl.ANY)


def dot_nt(a, b):
    return lax.dot_general(a, b, (((1,), (1,)), ((), ())), preferred_element_type=F32)


def grant(mib):
    return pltpu.CompilerParams(vmem_limit_bytes=mib << 20)


def pack_kernel(place, valid_len, span_ids, offset, keys_in, values_in, new_keys_in, new_values_in, *refs):
    outs, (keys, values, new_keys, new_values, heads, sems) = refs[:4], refs[4:]
    copies = [
        pltpu.make_async_copy(source, target, sems.at[i])
        for i, (source, target) in enumerate(
            ((keys_in, keys), (values_in, values), (new_keys_in, new_keys), (new_values_in, new_values))
        )
    ]
    for copy in copies:
        copy.start()
    slots = valid_len.shape[0]
    rows = slots * SPAN
    fresh = new_keys.shape[0]
    row_id = lax.broadcasted_iota(jnp.int32, (SPAN, HD), 0)
    lane_id = lax.broadcasted_iota(jnp.int32, (16, HD), 1)
    live = [
        jnp.clip(jnp.minimum(valid_len[s], offset[0] - span_ids[s] * SPAN), 0, SPAN) for s in range(slots)
    ]
    counts = jnp.zeros((16, HD), F32)
    for s in range(slots):
        counts = jnp.where(lane_id == s, live[s].astype(F32), counts)
    for copy in copies:
        copy.wait()
    for head in range(2):
        cols = slice(head * HD, (head + 1) * HD)
        for s in range(slots):
            part = slice(s * SPAN, (s + 1) * SPAN)
            visible = row_id < live[s]
            key = keys[part, cols].astype(F32)
            key = jnp.where(visible, key, jnp.broadcast_to(key[:1], key.shape))
            heads[head, 0, part, :] = key.astype(BF16)
            heads[head, 1, part, :] = jnp.where(visible, values[part, cols].astype(F32), 0.0).astype(BF16)
        heads[head, 0, rows : rows + fresh, :] = new_keys[:, cols]
        heads[head, 1, rows : rows + fresh, :] = new_values[:, cols]
        heads[head, 0, rows + fresh :, :] = counts.astype(BF16)
        heads[head, 1, rows + fresh :, :] = counts.astype(BF16)
    for k, out in enumerate(outs):
        out[...] = heads[lax.rem(place[0] + k, 4) // 2]


def attend_kernel(live, queries, kv0, kv1, kv2, kv3, pos_q, pos_n, out, kc, vc, top, acc):
    sources = (kv0, kv1, kv2, kv3)
    slots = live.shape[0] // len(sources)
    rows = slots * SPAN
    fresh = kv0.shape[1] - rows - 16
    heads = queries.shape[1] // HD
    tokens = queries.shape[0]
    row_id = lax.broadcasted_iota(jnp.int32, (SPAN, HD), 0)
    start = len(sources) * fresh

    def rounded(count):
        return ((count + 15) // 16) * 16

    place = jnp.int32(start)
    for i, kv in enumerate(sources):
        target = slice(i * fresh, (i + 1) * fresh)
        kc[target, :] = kv[0, rows : rows + fresh, :]
        vc[target, :HD] = kv[1, rows : rows + fresh, :]
        vc[target, HD:] = jnp.ones((fresh, HD), BF16)

        def gather_slot(s, at, kv=kv, i=i):
            count = live[i * slots + s]
            source = pl.ds(pl.multiple_of(s * SPAN, SPAN), SPAN)
            target = pl.ds(pl.multiple_of(at, 16), SPAN)
            kc[target, :] = kv[0, source, :]
            vc[target, :HD] = kv[1, source, :]
            vc[target, HD:] = jnp.where(row_id < count, 1.0, 0.0).astype(BF16)
            return at + rounded(count)

        place = lax.fori_loop(0, slots, gather_slot, place)
    tail = pl.ds(pl.multiple_of(place, 16), KEY_BLOCK)
    spare = kc[start : start + 16, :].astype(F32)[:1]
    spare = jnp.where(place > start, spare, 0.0)
    kc[tail, :] = jnp.broadcast_to(spare, (KEY_BLOCK, HD)).astype(BF16)
    vc[tail, :] = jnp.zeros((KEY_BLOCK, 2 * HD), BF16)
    blocks = (place + KEY_BLOCK - 1) // KEY_BLOCK

    lane_id = lax.broadcasted_iota(jnp.int32, (tokens, HD), 1)
    key_id = lax.broadcasted_iota(jnp.int32, (1, KEY_BLOCK), 1)
    seen = jnp.where(key_id < place, pos_n[...], tokens) <= pos_q[...]
    lanes = [slice(j * HD, (j + 1) * HD) for j in range(KEY_BLOCK // HD)]

    def head_cols(h):
        return slice(h * HD, (h + 1) * HD)

    def rounded_max(s):
        high = functools.reduce(jnp.maximum, [s[:, g] for g in lanes])
        m = jnp.maximum(jnp.max(high, axis=1, keepdims=True) * LOG2_SCALE, LOWEST)
        return jnp.broadcast_to(m.astype(BF16).astype(F32), (tokens, HD))

    def score(h, part):
        return dot_nt(queries[:, head_cols(h)], kc[part, :])

    def sums(s, m, part):
        p = jnp.concatenate([jnp.exp2(s[:, g] * LOG2_SCALE - m).astype(BF16) for g in lanes], axis=1)
        return jnp.dot(p, vc[part, :], preferred_element_type=F32)

    def begin(h, part, s):
        s = jnp.where(seen, s, FILL)
        m = rounded_max(s)
        top[h] = m
        acc[h] = sums(s, m, part)

    def add(h, part, s):
        old = top[h]
        m = jnp.maximum(old, rounded_max(s))
        top[h] = m
        shrink = jnp.exp2(old - m)
        term = sums(s, m, part)
        acc[h, :, :HD] = acc[h, :, :HD] * shrink + term[:, :HD]
        acc[h, :, HD:] = acc[h, :, HD:] * shrink + term[:, HD:]

    def every_head(visit, part):
        s = score(0, part)
        for h in range(heads):
            following = score(h + 1, part) if h + 1 < heads else None
            visit(h, part, s)
            s = following

    every_head(begin, slice(0, KEY_BLOCK))

    def step(b, _):
        every_head(add, pl.ds(pl.multiple_of(b * KEY_BLOCK, KEY_BLOCK), KEY_BLOCK))
        return _

    lax.fori_loop(1, blocks, step, 0)

    notes = jnp.zeros((tokens, HD), F32)
    for h in range(heads):
        total = acc[h, :, HD:]
        high = total.astype(BF16).astype(F32)
        out[:, head_cols(h)] = acc[h, :, :HD].astype(BF16)
        notes = jnp.where(lane_id == h, top[h], notes)
        notes = jnp.where(lane_id == heads + h, high, notes)
        notes = jnp.where(lane_id == 2 * heads + h, total - high, notes)
    out[:, heads * HD :] = notes.astype(BF16)


def settle_kernel(parts, out):
    groups, tokens, width = parts.shape
    heads = width // HD - 1
    notes = [parts[g, :, heads * HD :].astype(F32) for g in range(groups)]
    highest = notes[0]
    for g in range(1, groups):
        highest = jnp.maximum(highest, notes[g])
    factors = [jnp.exp2(notes[g] - highest) for g in range(groups)]
    for h in range(heads):
        cols = slice(h * HD, (h + 1) * HD)
        numerator = jnp.zeros((tokens, HD), F32)
        total = jnp.zeros((tokens, 1), F32)
        for g in range(groups):
            factor = factors[g][:, h : h + 1]
            numerator += factor * parts[g, :, cols].astype(F32)
            total += factor * (
                notes[g][:, heads + h : heads + h + 1] + notes[g][:, 2 * heads + h : 2 * heads + h + 1]
            )
        attended = (numerator / total).astype(BF16)
        for g in range(out.shape[0]):
            out[g, :, cols] = attended


def cut_kernel(place, weight, *refs):
    outs, (held, arrived, left) = refs[:-3], refs[-3:]
    rows = held.shape[1]
    copies = []
    for i, out in enumerate(outs):
        k, start = i // PIECES, sum(o.shape[0] for o in outs[i // PIECES * PIECES : i])
        page = held.at[k, slice(start, start + out.shape[0]), :]
        part = pl.ds(pl.multiple_of(lax.rem(place[0] + k, 4) * rows + start, 16), out.shape[0])
        copies.append(
            (
                pltpu.make_async_copy(weight.at[part, :], page, arrived.at[i]),
                pltpu.make_async_copy(page, out, left.at[i]),
            )
        )
        copies[i][0].start()
    for arrival, departure in copies:
        arrival.wait()
        departure.start()
    for _, departure in copies:
        departure.wait()


def project_kernel(place, attended, *refs):
    weights, out = refs[:-1], refs[-1]
    size = out.shape[2]
    picked = [pl.ds(pl.multiple_of((2 * r + place[1]) * size, size), size) for r in range(out.shape[1])]
    rows = jnp.concatenate([attended[p, :] for p in picked], axis=0)
    for k in range(4):
        target = lax.rem(place[0] + 4 - k, 4)
        weight = jnp.concatenate([w[...] for w in weights[k * PIECES : (k + 1) * PIECES]], axis=0)
        term = jnp.dot(rows, weight, preferred_element_type=F32).astype(BF16)
        for r in range(out.shape[1]):
            out[target, r] = term[r * size : (r + 1) * size]


def swap(x, axes):
    return lax.all_to_all(x, axes, split_axis=0, concat_axis=0, tiled=False)


def along_y(x, distance):
    return lax.ppermute(x, "y", [(i, (i + distance) % 4) for i in range(4)])


def to_other(x, axis):
    return lax.ppermute(x, axis, [(0, 1), (1, 0)])


def shards(
    queries,
    new_keys,
    new_values,
    cache_keys,
    cache_values,
    span_ids,
    valid_len,
    pos_ids,
    offset,
    out_weight,
):
    y, core = lax.axis_index("y"), lax.axis_index("core")
    group = lax.axis_index("z") * 2 + lax.axis_index("x_hi")
    place = y[None].astype(jnp.int32)
    groups = 8
    fresh, width = queries.shape
    slots = span_ids.shape[0]
    rows = slots * SPAN
    quarter = width // 4
    tokens = pos_ids.shape[0]

    packet = jax.ShapeDtypeStruct((2, rows + fresh + 16, HD), BF16)
    with jax.named_scope("pack"):
        packets = pl.pallas_call(
            pack_kernel,
            out_shape=[packet] * 4,
            in_specs=[SMEM] * 4 + [ANY] * 4,
            out_specs=[VMEM] * 4,
            scratch_shapes=[
                pltpu.VMEM(cache_keys.shape, BF16),
                pltpu.VMEM(cache_keys.shape, BF16),
                pltpu.VMEM(new_keys.shape, BF16),
                pltpu.VMEM(new_keys.shape, BF16),
                pltpu.VMEM((2,) + packet.shape, BF16),
                pltpu.SemaphoreType.DMA((4,)),
            ],
            compiler_params=grant(56),
            cost_estimate=TINY,
        )(place, valid_len, span_ids, offset, cache_keys, cache_values, new_keys, new_values)
    with jax.named_scope("move_queries"):
        mine = swap(queries.reshape(fresh, 4, quarter).transpose(1, 0, 2), "y")
        mine, packets = lax.optimization_barrier((mine, packets))
        mine = mine.reshape(4 * fresh, quarter)
        mine = swap(jnp.broadcast_to(mine[None], (groups,) + mine.shape), ("z", "x_hi")).reshape(tokens, quarter)
    with jax.named_scope("move_kv"):
        kv = [packets[0]] + [along_y(packets[k], k) for k in range(1, 4)]
        all_live = jnp.stack([packet[0, rows + fresh, :slots] for packet in kv]).astype(jnp.int32).reshape(-1)

    columns = out_weight.shape[1]
    with jax.named_scope("move_weight"):
        sizes = (448, 288, 288)
        chunks = pl.pallas_call(
            cut_kernel,
            out_shape=[jax.ShapeDtypeStruct((size, columns), BF16) for size in sizes * 4],
            in_specs=[SMEM, ANY],
            out_specs=[ANY] * (4 * PIECES),
            scratch_shapes=[
                pltpu.VMEM((4, quarter, columns), BF16),
                pltpu.SemaphoreType.DMA((4 * PIECES,)),
                pltpu.SemaphoreType.DMA((4 * PIECES,)),
            ],
            compiler_params=grant(56),
            cost_estimate=TINY,
        )(place, lax.optimization_barrier((out_weight, packets))[0])

        def pieces(j, after):
            ready, _ = lax.optimization_barrier(([chunks[k * PIECES + j] for k in range(4)], after))
            return [ready[0]] + [along_y(ready[k], k) for k in range(1, 4)]

        weights = [pieces(j, kv) for j in range(PIECES)]
        mine, chunks = lax.optimization_barrier((mine, chunks))

    pos_n = [
        lax.dynamic_slice_in_dim(pos_ids, (group * 4 + lax.rem(y + 4 - k, 4)) * fresh, fresh) for k in range(4)
    ]
    pos_n = jnp.concatenate(pos_n + [jnp.full((KEY_BLOCK - 4 * fresh,), -1, jnp.int32)])[None]
    pos_q = pos_ids[:, None]

    capacity = 4 * (rows + fresh) + KEY_BLOCK
    heads = quarter // HD
    with jax.named_scope("attend"):
        partial = pl.pallas_call(
            attend_kernel,
            out_shape=jax.ShapeDtypeStruct((tokens, quarter + HD), BF16),
            in_specs=[SMEM] + [VMEM] * 7,
            out_specs=VMEM,
            scratch_shapes=[
                pltpu.VMEM((capacity, HD), BF16),
                pltpu.VMEM((capacity, 2 * HD), BF16),
                pltpu.VMEM((heads, tokens, HD), F32),
                pltpu.VMEM((heads, tokens, 2 * HD), F32),
            ],
            compiler_params=grant(40),
            cost_estimate=TINY,
        )(all_live, mine, *kv, pos_q, pos_n)

    with jax.named_scope("move_partials"):
        partial, weights[0] = lax.optimization_barrier((partial, weights[0]))
        partial = swap(partial.reshape(groups, tokens // groups, quarter + HD), ("z", "x_hi"))
    with jax.named_scope("settle"):
        attended = pl.pallas_call(
            settle_kernel,
            out_shape=jax.ShapeDtypeStruct((groups, tokens // groups, quarter), BF16),
            in_specs=[VMEM],
            out_specs=VMEM,
            compiler_params=grant(24),
            cost_estimate=TINY,
        )(partial)
    with jax.named_scope("move_attended"):
        attended, weights[1] = lax.optimization_barrier((attended, weights[1]))
        attended = swap(attended, ("z", "x_hi")).reshape(tokens, quarter)


    def project(which):
        return pl.pallas_call(
            project_kernel,
            out_shape=jax.ShapeDtypeStruct((4, 2, tokens // 4, columns), BF16),
            in_specs=[SMEM] + [VMEM] * (1 + 4 * PIECES),
            out_specs=VMEM,
            compiler_params=grant(32),
            cost_estimate=TINY,
        )(jnp.stack([y, which]).astype(jnp.int32), attended, *[w[k] for k in range(4) for w in weights])

    with jax.named_scope("project"):
        theirs = to_other(project(1 - core), "core")
        terms = (project(core).astype(F32) + theirs.astype(F32)).astype(BF16)
    with jax.named_scope("move_terms"):
        terms = swap(terms.reshape(8, tokens // 4, columns), ("y", "x_lo"))
    return jnp.sum(terms.astype(F32), axis=0).astype(BF16)


def solution(mesh):
    fine = Mesh(mesh.devices.reshape(4, 2, 4, 2, 2), ("z", "x_hi", "y", "x_lo", "core"))
    ctx, head = ("z", "x_hi", "y"), ("x_lo", "core")
    in_specs = (
        P(ctx, head),
        P(ctx, head),
        P(ctx, head),
        P(ctx, head),
        P(ctx, head),
        P(ctx),
        P(ctx),
        P(),
        P(),
        P(head, ctx),
    )
    return jax.shard_map(shards, mesh=fine, in_specs=in_specs, out_specs=P(head, ctx), check_vma=False)
```

```python
import functools
import math

import jax
import jax.numpy as jnp
import numpy as np
from jax import lax
from jax.experimental import pallas as pl
from jax.experimental.pallas import tpu as pltpu
from jax.sharding import Mesh
from jax.sharding import PartitionSpec as P

HD = 128
SPAN = 128
KEY_BLOCK = 512
PIECES = 3
FILL = -1e30
LOWEST = -1e20
LOG2_SCALE = math.log2(math.e) / math.sqrt(HD)
F32 = jnp.float32
BF16 = jnp.bfloat16
TINY = pl.CostEstimate(flops=1, bytes_accessed=1, transcendentals=0)
VMEM = pl.BlockSpec(memory_space=pltpu.VMEM)
SMEM = pl.BlockSpec(memory_space=pltpu.SMEM)
ANY = pl.BlockSpec(memory_space=pl.ANY)


def dot_nt(a, b):
    return lax.dot_general(a, b, (((1,), (1,)), ((), ())), preferred_element_type=F32)


def grant(mib):
    return pltpu.CompilerParams(vmem_limit_bytes=mib << 20)


def pack_kernel(place, valid_len, span_ids, offset, pos_ids, keys_in, values_in, new_keys_in, new_values_in, *refs):
    outs, (keys, values, new_keys, new_values, heads, sems) = refs[:4], refs[4:]
    copies = [
        pltpu.make_async_copy(source, target, sems.at[i])
        for i, (source, target) in enumerate(
            ((keys_in, keys), (values_in, values), (new_keys_in, new_keys), (new_values_in, new_values))
        )
    ]
    for copy in copies:
        copy.start()
    slots = valid_len.shape[0]
    rows = slots * SPAN
    fresh = new_keys.shape[0]
    row_id = lax.broadcasted_iota(jnp.int32, (SPAN, HD), 0)
    lane_id = lax.broadcasted_iota(jnp.int32, (16, HD), 1)
    live = [
        jnp.clip(jnp.minimum(valid_len[s], offset[0] - span_ids[s] * SPAN), 0, SPAN) for s in range(slots)
    ]
    counts = jnp.zeros((16, HD), F32)
    for s in range(slots):
        counts = jnp.where(lane_id == s, live[s].astype(F32), counts)
    for j in range(fresh):
        position = pos_ids[place[1] * fresh + j]
        counts = jnp.where(lane_id == fresh + j, (position >> 4).astype(F32), counts)
        counts = jnp.where(lane_id == 2 * fresh + j, (position & 15).astype(F32), counts)
    for copy in copies:
        copy.wait()
    for head in range(2):
        cols = slice(head * HD, (head + 1) * HD)
        for s in range(slots):
            part = slice(s * SPAN, (s + 1) * SPAN)
            visible = row_id < live[s]
            key = keys[part, cols].astype(F32)
            key = jnp.where(visible, key, jnp.broadcast_to(key[:1], key.shape))
            heads[head, 0, part, :] = key.astype(BF16)
            heads[head, 1, part, :] = jnp.where(visible, values[part, cols].astype(F32), 0.0).astype(BF16)
        heads[head, 0, rows : rows + fresh, :] = new_keys[:, cols]
        heads[head, 1, rows : rows + fresh, :] = new_values[:, cols]
        heads[head, 0, rows + fresh :, :] = counts.astype(BF16)
        heads[head, 1, rows + fresh :, :] = counts.astype(BF16)
    for k, out in enumerate(outs):
        out[...] = heads[lax.rem(place[0] + k, 4) // 2]


def attend_kernel(queries, kv0, kv1, kv2, kv3, pos_q, out, kc, vc, top, acc, held, table, live, sems):
    sources = (kv0, kv1, kv2, kv3)
    copies = [pltpu.make_async_copy(kv, held.at[i], sems.at[i]) for i, kv in enumerate(sources)]
    for copy in copies:
        copy.start()
    fresh = 16
    rows = kv0.shape[1] - 2 * fresh
    slots = rows // SPAN
    heads = queries.shape[1] // HD
    tokens = queries.shape[0]
    row_id = lax.broadcasted_iota(jnp.int32, (SPAN, HD), 0)
    start = len(sources) * fresh

    def rounded(count):
        return ((count + 15) // 16) * 16

    for copy in copies:
        copy.wait()
    notes = [held[i, 0, rows + fresh :, :].astype(F32) for i in range(len(sources))]
    for i, note in enumerate(notes):
        table[i] = note[:8].astype(jnp.int32)
    counts = pltpu.make_async_copy(table, live, sems.at[len(sources)])
    counts.start()
    lane = lax.broadcasted_iota(jnp.int32, (8, HD), 1)
    pos_fresh = jnp.full((8, HD), -1.0, F32)
    for i, note in enumerate(notes):
        high = pltpu.roll(note[:8], (i - 1) * fresh % HD, 1)
        low = pltpu.roll(note[:8], (i - 2) * fresh % HD, 1)
        pos_fresh = jnp.where(lane // fresh == i, high * 16.0 + low, pos_fresh)
    pos_column = jnp.transpose(jnp.broadcast_to(pos_q[...].astype(F32), (HD, tokens)))
    counts.wait()
    place = jnp.int32(start)
    for i in range(len(sources)):
        kv = held.at[i]
        target = slice(i * fresh, (i + 1) * fresh)
        kc[target, :] = kv[0, rows : rows + fresh, :]
        vc[target, :HD] = kv[1, rows : rows + fresh, :]
        vc[target, HD:] = jnp.ones((fresh, HD), BF16)

        def gather_slot(s, at, kv=kv, i=i):
            count = live[i, 0, s]
            source = pl.ds(pl.multiple_of(s * SPAN, SPAN), SPAN)
            target = pl.ds(pl.multiple_of(at, 16), SPAN)
            kc[target, :] = kv[0, source, :]
            vc[target, :HD] = kv[1, source, :]
            vc[target, HD:] = jnp.where(row_id < count, 1.0, 0.0).astype(BF16)
            return at + rounded(count)

        place = lax.fori_loop(0, slots, gather_slot, place)
    tail = pl.ds(pl.multiple_of(place, 16), KEY_BLOCK)
    spare = kc[start : start + 16, :].astype(F32)[:1]
    spare = jnp.where(place > start, spare, 0.0)
    kc[tail, :] = jnp.broadcast_to(spare, (KEY_BLOCK, HD)).astype(BF16)
    vc[tail, :] = jnp.zeros((KEY_BLOCK, 2 * HD), BF16)
    blocks = (place + KEY_BLOCK - 1) // KEY_BLOCK

    lane_id = lax.broadcasted_iota(jnp.int32, (tokens, HD), 1)
    lanes = [slice(j * HD, (j + 1) * HD) for j in range(KEY_BLOCK // HD)]
    pos_key = [
        jnp.where(lane[:1] + j * HD < place, pos_fresh[:1] if j == 0 else -1.0, float(tokens))
        for j in range(KEY_BLOCK // HD)
    ]

    def head_cols(h):
        return slice(h * HD, (h + 1) * HD)

    def rounded_max(s):
        high = functools.reduce(jnp.maximum, [s[:, g] for g in lanes])
        m = jnp.maximum(jnp.max(high, axis=1, keepdims=True) * LOG2_SCALE, LOWEST)
        return jnp.broadcast_to(m.astype(BF16).astype(F32), (tokens, HD))

    def score(h, part):
        return dot_nt(queries[:, head_cols(h)], kc[part, :])

    def sums(s, m, part):
        p = jnp.concatenate([jnp.exp2(s[:, g] * LOG2_SCALE - m).astype(BF16) for g in lanes], axis=1)
        return jnp.dot(p, vc[part, :], preferred_element_type=F32)

    def begin(h, part, s):
        s = jnp.concatenate([jnp.where(p <= pos_column, s[:, g], FILL) for p, g in zip(pos_key, lanes)], axis=1)
        m = rounded_max(s)
        top[h] = m
        acc[h] = sums(s, m, part)

    def add(h, part, s):
        old = top[h]
        m = jnp.maximum(old, rounded_max(s))
        top[h] = m
        shrink = jnp.exp2(old - m)
        term = sums(s, m, part)
        acc[h, :, :HD] = acc[h, :, :HD] * shrink + term[:, :HD]
        acc[h, :, HD:] = acc[h, :, HD:] * shrink + term[:, HD:]

    def every_head(visit, part):
        s = score(0, part)
        for h in range(heads):
            following = score(h + 1, part) if h + 1 < heads else None
            visit(h, part, s)
            s = following

    every_head(begin, slice(0, KEY_BLOCK))

    def step(b, _):
        every_head(add, pl.ds(pl.multiple_of(b * KEY_BLOCK, KEY_BLOCK), KEY_BLOCK))
        return _

    lax.fori_loop(1, blocks, step, 0)

    notes = jnp.zeros((tokens, HD), F32)
    for h in range(heads):
        total = acc[h, :, HD:]
        high = total.astype(BF16).astype(F32)
        out[:, head_cols(h)] = acc[h, :, :HD].astype(BF16)
        notes = jnp.where(lane_id == h, top[h], notes)
        notes = jnp.where(lane_id == heads + h, high, notes)
        notes = jnp.where(lane_id == 2 * heads + h, total - high, notes)
    out[:, heads * HD :] = notes.astype(BF16)


def settle_kernel(parts, out):
    groups, tokens, width = parts.shape
    heads = width // HD - 1
    lane_id = lax.broadcasted_iota(jnp.int32, (tokens, HD), 1)
    notes = [parts[g, :, heads * HD :].astype(F32) for g in range(groups)]
    highest = functools.reduce(jnp.maximum, notes)
    factors = [jnp.exp2(jnp.where(lane_id < heads, n - highest, 0.0)) for n in notes]
    total = 0.0
    for factor, n in zip(factors, notes):
        total += factor * (pltpu.roll(n, HD - heads, 1) + pltpu.roll(n, HD - 2 * heads, 1))
    shares = [factor / jnp.where(lane_id < heads, total, 1.0) for factor in factors]
    for h in range(heads):
        cols = slice(h * HD, (h + 1) * HD)
        attended = 0.0
        for g in range(groups):
            attended += shares[g][:, h : h + 1] * parts[g, :, cols].astype(F32)
        attended = attended.astype(BF16)
        for g in range(out.shape[0]):
            out[g, :, cols] = attended


def cut_kernel(place, weight, *refs):
    outs, (held, arrived, left) = refs[:-3], refs[-3:]
    rows = held.shape[1]
    copies = []
    for i, out in enumerate(outs):
        k, start = i // PIECES, sum(o.shape[0] for o in outs[i // PIECES * PIECES : i])
        page = held.at[k, slice(start, start + out.shape[0]), :]
        part = pl.ds(pl.multiple_of(lax.rem(place[0] + k, 4) * rows + start, 16), out.shape[0])
        copies.append(
            (
                pltpu.make_async_copy(weight.at[part, :], page, arrived.at[i]),
                pltpu.make_async_copy(page, out, left.at[i]),
            )
        )
        copies[i][0].start()
    for arrival, departure in copies:
        arrival.wait()
        departure.start()
    for _, departure in copies:
        departure.wait()


def project_kernel(place, attended, *refs):
    weights, out = refs[:-1], refs[-1]
    size = out.shape[2]
    picked = [pl.ds(pl.multiple_of((2 * r + place[1]) * size, size), size) for r in range(out.shape[1])]
    rows = jnp.concatenate([attended[p, :] for p in picked], axis=0)
    for k in range(4):
        target = lax.rem(place[0] + 4 - k, 4)
        term, start = 0.0, 0
        for w in weights[k * PIECES : (k + 1) * PIECES]:
            term += jnp.dot(rows[:, start : start + w.shape[0]], w[...], preferred_element_type=F32)
            start += w.shape[0]
        term = term.astype(BF16)
        for r in range(out.shape[1]):
            out[target, r] = term[r * size : (r + 1) * size]


def swap(x, axes):
    return lax.all_to_all(x, axes, split_axis=0, concat_axis=0, tiled=False)


def along_y(x, distance):
    return lax.ppermute(x, "y", [(i, (i + distance) % 4) for i in range(4)])


def to_other(x, axis):
    return lax.ppermute(x, axis, [(0, 1), (1, 0)])


def shards(
    queries,
    new_keys,
    new_values,
    cache_keys,
    cache_values,
    span_ids,
    valid_len,
    pos_ids,
    offset,
    out_weight,
):
    y, core = lax.axis_index("y"), lax.axis_index("core")
    group = lax.axis_index("z") * 2 + lax.axis_index("x_hi")
    place = y[None].astype(jnp.int32)
    groups = 8
    fresh, width = queries.shape
    slots = span_ids.shape[0]
    rows = slots * SPAN
    quarter = width // 4
    tokens = pos_ids.shape[0]

    packet = jax.ShapeDtypeStruct((2, rows + fresh + 16, HD), BF16)
    with jax.named_scope("pack"):
        packets = pl.pallas_call(
            pack_kernel,
            out_shape=[packet] * 4,
            in_specs=[SMEM] * 5 + [ANY] * 4,
            out_specs=[VMEM] * 4,
            scratch_shapes=[
                pltpu.VMEM(cache_keys.shape, BF16),
                pltpu.VMEM(cache_keys.shape, BF16),
                pltpu.VMEM(new_keys.shape, BF16),
                pltpu.VMEM(new_keys.shape, BF16),
                pltpu.VMEM((2,) + packet.shape, BF16),
                pltpu.SemaphoreType.DMA((4,)),
            ],
            compiler_params=grant(56),
            cost_estimate=TINY,
        )(jnp.stack([y, group * 4 + y]).astype(jnp.int32), valid_len, span_ids, offset, pos_ids, cache_keys, cache_values, new_keys, new_values)
    with jax.named_scope("move_queries"):
        mine = swap(queries.reshape(fresh, 4, quarter).transpose(1, 0, 2), "y")
        mine, packets = lax.optimization_barrier((mine, packets))
        mine = mine.reshape(4 * fresh, quarter)
        mine = swap(jnp.broadcast_to(mine[None], (groups,) + mine.shape), ("z", "x_hi")).reshape(tokens, quarter)
    with jax.named_scope("move_kv"):
        kv = [packets[0]] + [along_y(packets[k], k) for k in range(1, 4)]

    columns = out_weight.shape[1]
    with jax.named_scope("move_weight"):
        sizes = (448, 320, 256)
        chunks = pl.pallas_call(
            cut_kernel,
            out_shape=[jax.ShapeDtypeStruct((size, columns), BF16) for size in sizes * 4],
            in_specs=[SMEM, ANY],
            out_specs=[ANY] * (4 * PIECES),
            scratch_shapes=[
                pltpu.VMEM((4, quarter, columns), BF16),
                pltpu.SemaphoreType.DMA((4 * PIECES,)),
                pltpu.SemaphoreType.DMA((4 * PIECES,)),
            ],
            compiler_params=grant(56),
            cost_estimate=TINY,
        )(place, lax.optimization_barrier((out_weight, packets))[0])

        def pieces(j):
            ready, _ = lax.optimization_barrier(([chunks[k * PIECES + j] for k in range(4)], kv[1:3]))
            return [ready[0]] + [along_y(ready[k], k) for k in range(1, 4)]

        weights = [pieces(j) for j in range(PIECES)]
        mine, chunks = lax.optimization_barrier((mine, chunks))

    capacity = 4 * (rows + fresh) + KEY_BLOCK
    heads = quarter // HD
    with jax.named_scope("attend"):
        partial = pl.pallas_call(
            attend_kernel,
            out_shape=jax.ShapeDtypeStruct((tokens, quarter + HD), BF16),
            in_specs=[VMEM] + [ANY] * 4 + [VMEM],
            out_specs=VMEM,
            scratch_shapes=[
                pltpu.VMEM((capacity, HD), BF16),
                pltpu.VMEM((capacity, 2 * HD), BF16),
                pltpu.VMEM((heads, tokens, HD), F32),
                pltpu.VMEM((heads, tokens, 2 * HD), F32),
                pltpu.VMEM((4,) + packet.shape, BF16),
                pltpu.VMEM((4, 8, HD), jnp.int32),
                pltpu.SMEM((4, 8, HD), jnp.int32),
                pltpu.SemaphoreType.DMA((5,)),
            ],
            compiler_params=grant(24),
            cost_estimate=TINY,
        )(mine, *kv, pos_ids[None])

    with jax.named_scope("move_partials"):
        partial, weights[0] = lax.optimization_barrier((partial, weights[0]))
        partial = swap(partial.reshape(groups, tokens // groups, quarter + HD), ("z", "x_hi"))
    with jax.named_scope("settle"):
        attended = pl.pallas_call(
            settle_kernel,
            out_shape=jax.ShapeDtypeStruct((groups, tokens // groups, quarter), BF16),
            in_specs=[VMEM],
            out_specs=VMEM,
            compiler_params=grant(24),
            cost_estimate=TINY,
        )(partial)
    with jax.named_scope("move_attended"):
        attended, weights[1] = lax.optimization_barrier((attended, weights[1]))
        attended = swap(attended, ("z", "x_hi")).reshape(tokens, quarter)


    def project(which):
        return pl.pallas_call(
            project_kernel,
            out_shape=jax.ShapeDtypeStruct((4, 2, tokens // 4, columns), BF16),
            in_specs=[SMEM] + [VMEM] * (1 + 4 * PIECES),
            out_specs=VMEM,
            compiler_params=grant(32),
            cost_estimate=TINY,
        )(jnp.stack([y, which]).astype(jnp.int32), attended, *[w[k] for k in range(4) for w in weights])

    with jax.named_scope("project"):
        theirs = to_other(project(1 - core), "core")
        terms = (project(core).astype(F32) + theirs.astype(F32)).astype(BF16)
    with jax.named_scope("move_terms"):
        terms = swap(terms.reshape(8, tokens // 4, columns), ("y", "x_lo"))
    return jnp.sum(terms.astype(F32), axis=0).astype(BF16)


def solution(mesh):
    fine = Mesh(mesh.devices.reshape(4, 2, 4, 2, 2), ("z", "x_hi", "y", "x_lo", "core"))
    ctx, head = ("z", "x_hi", "y"), ("x_lo", "core")
    in_specs = (
        P(ctx, head),
        P(ctx, head),
        P(ctx, head),
        P(ctx, head),
        P(ctx, head),
        P(ctx),
        P(ctx),
        P(),
        P(),
        P(head, ctx),
    )
    return jax.shard_map(shards, mesh=fine, in_specs=in_specs, out_specs=P(head, ctx), check_vma=False)
```

```python
import functools
import math

import jax
import jax.numpy as jnp
import numpy as np
from jax import lax
from jax.experimental import pallas as pl
from jax.experimental.pallas import tpu as pltpu
from jax.sharding import Mesh
from jax.sharding import PartitionSpec as P

HD = 128
SPAN = 128
KEY_BLOCK = 512
PIECES = 3
FILL = -1e30
LOWEST = -1e20
LOG2_SCALE = math.log2(math.e) / math.sqrt(HD)
F32 = jnp.float32
BF16 = jnp.bfloat16
TINY = pl.CostEstimate(flops=1, bytes_accessed=1, transcendentals=0)
VMEM = pl.BlockSpec(memory_space=pltpu.VMEM)
SMEM = pl.BlockSpec(memory_space=pltpu.SMEM)
ANY = pl.BlockSpec(memory_space=pl.ANY)


def dot_nt(a, b):
    return lax.dot_general(a, b, (((1,), (1,)), ((), ())), preferred_element_type=F32)


def grant(mib):
    return pltpu.CompilerParams(vmem_limit_bytes=mib << 20)


def pack_kernel(place, valid_len, span_ids, offset, keys_in, values_in, new_keys_in, new_values_in, *refs):
    outs, (keys, values, new_keys, new_values, heads, sems) = refs[:4], refs[4:]
    copies = [
        pltpu.make_async_copy(source, target, sems.at[i])
        for i, (source, target) in enumerate(
            ((keys_in, keys), (values_in, values), (new_keys_in, new_keys), (new_values_in, new_values))
        )
    ]
    for copy in copies:
        copy.start()
    slots = valid_len.shape[0]
    rows = slots * SPAN
    fresh = new_keys.shape[0]
    row_id = lax.broadcasted_iota(jnp.int32, (SPAN, HD), 0)
    lane_id = lax.broadcasted_iota(jnp.int32, (16, HD), 1)
    live = [
        jnp.clip(jnp.minimum(valid_len[s], offset[0] - span_ids[s] * SPAN), 0, SPAN) for s in range(slots)
    ]
    counts = jnp.zeros((16, HD), F32)
    for s in range(slots):
        counts = jnp.where(lane_id == s, live[s].astype(F32), counts)
    for copy in copies:
        copy.wait()
    for head in range(2):
        cols = slice(head * HD, (head + 1) * HD)
        for s in range(slots):
            part = slice(s * SPAN, (s + 1) * SPAN)
            visible = row_id < live[s]
            key = keys[part, cols].astype(F32)
            key = jnp.where(visible, key, jnp.broadcast_to(key[:1], key.shape))
            heads[head, 0, part, :] = key.astype(BF16)
            heads[head, 1, part, :] = jnp.where(visible, values[part, cols].astype(F32), 0.0).astype(BF16)
        heads[head, 0, rows : rows + fresh, :] = new_keys[:, cols]
        heads[head, 1, rows : rows + fresh, :] = new_values[:, cols]
        heads[head, 0, rows + fresh :, :] = counts.astype(BF16)
        heads[head, 1, rows + fresh :, :] = counts.astype(BF16)
    for k, out in enumerate(outs):
        out[...] = heads[lax.rem(place[0] + k, 4) // 2]


def attend_kernel(live, queries, kv0, kv1, kv2, kv3, pos_q, pos_n, out, kc, vc, top, acc):
    sources = (kv0, kv1, kv2, kv3)
    slots = live.shape[0] // len(sources)
    rows = slots * SPAN
    fresh = kv0.shape[1] - rows - 16
    heads = queries.shape[1] // HD
    tokens = queries.shape[0]
    row_id = lax.broadcasted_iota(jnp.int32, (SPAN, HD), 0)
    start = len(sources) * fresh

    def rounded(count):
        return ((count + 15) // 16) * 16

    place = jnp.int32(start)
    for i, kv in enumerate(sources):
        target = slice(i * fresh, (i + 1) * fresh)
        kc[target, :] = kv[0, rows : rows + fresh, :]
        vc[target, :HD] = kv[1, rows : rows + fresh, :]
        vc[target, HD:] = jnp.ones((fresh, HD), BF16)

        def gather_slot(s, at, kv=kv, i=i):
            count = live[i * slots + s]
            source = pl.ds(pl.multiple_of(s * SPAN, SPAN), SPAN)
            target = pl.ds(pl.multiple_of(at, 16), SPAN)
            kc[target, :] = kv[0, source, :]
            vc[target, :HD] = kv[1, source, :]
            vc[target, HD:] = jnp.where(row_id < count, 1.0, 0.0).astype(BF16)
            return at + rounded(count)

        place = lax.fori_loop(0, slots, gather_slot, place)
    tail = pl.ds(pl.multiple_of(place, 16), KEY_BLOCK)
    spare = kc[start : start + 16, :].astype(F32)[:1]
    spare = jnp.where(place > start, spare, 0.0)
    kc[tail, :] = jnp.broadcast_to(spare, (KEY_BLOCK, HD)).astype(BF16)
    vc[tail, :] = jnp.zeros((KEY_BLOCK, 2 * HD), BF16)
    blocks = (place + KEY_BLOCK - 1) // KEY_BLOCK

    lane_id = lax.broadcasted_iota(jnp.int32, (tokens, HD), 1)
    key_id = lax.broadcasted_iota(jnp.int32, (1, KEY_BLOCK), 1)
    seen = jnp.where(key_id < place, pos_n[...], tokens) <= pos_q[...]
    lanes = [slice(j * HD, (j + 1) * HD) for j in range(KEY_BLOCK // HD)]

    def head_cols(h):
        return slice(h * HD, (h + 1) * HD)

    def rounded_max(s):
        high = functools.reduce(jnp.maximum, [s[:, g] for g in lanes])
        m = jnp.maximum(jnp.max(high, axis=1, keepdims=True) * LOG2_SCALE, LOWEST)
        return jnp.broadcast_to(m.astype(BF16).astype(F32), (tokens, HD))

    def score(h, part):
        return dot_nt(queries[:, head_cols(h)], kc[part, :])

    def sums(s, m, part):
        p = jnp.concatenate([jnp.exp2(s[:, g] * LOG2_SCALE - m).astype(BF16) for g in lanes], axis=1)
        return jnp.dot(p, vc[part, :], preferred_element_type=F32)

    def begin(h, part, s):
        s = jnp.where(seen, s, FILL)
        m = rounded_max(s)
        top[h] = m
        acc[h] = sums(s, m, part)

    def add(h, part, s):
        old = top[h]
        m = jnp.maximum(old, rounded_max(s))
        top[h] = m
        shrink = jnp.exp2(old - m)
        term = sums(s, m, part)
        acc[h, :, :HD] = acc[h, :, :HD] * shrink + term[:, :HD]
        acc[h, :, HD:] = acc[h, :, HD:] * shrink + term[:, HD:]

    def every_head(visit, part):
        s = score(0, part)
        for h in range(heads):
            following = score(h + 1, part) if h + 1 < heads else None
            visit(h, part, s)
            s = following

    every_head(begin, slice(0, KEY_BLOCK))

    def step(b, _):
        every_head(add, pl.ds(pl.multiple_of(b * KEY_BLOCK, KEY_BLOCK), KEY_BLOCK))
        return _

    lax.fori_loop(1, blocks, step, 0)

    notes = jnp.zeros((tokens, HD), F32)
    for h in range(heads):
        total = acc[h, :, HD:]
        high = total.astype(BF16).astype(F32)
        out[:, head_cols(h)] = acc[h, :, :HD].astype(BF16)
        notes = jnp.where(lane_id == h, top[h], notes)
        notes = jnp.where(lane_id == heads + h, high, notes)
        notes = jnp.where(lane_id == 2 * heads + h, total - high, notes)
    out[:, heads * HD :] = notes.astype(BF16)


def settle_kernel(parts, out):
    groups, tokens, width = parts.shape
    heads = width // HD - 1
    lane_id = lax.broadcasted_iota(jnp.int32, (tokens, HD), 1)
    notes = [parts[g, :, heads * HD :].astype(F32) for g in range(groups)]
    highest = functools.reduce(jnp.maximum, notes)
    factors = [jnp.exp2(jnp.where(lane_id < heads, n - highest, 0.0)) for n in notes]
    total = 0.0
    for factor, n in zip(factors, notes):
        total += factor * (pltpu.roll(n, HD - heads, 1) + pltpu.roll(n, HD - 2 * heads, 1))
    shares = [factor / jnp.where(lane_id < heads, total, 1.0) for factor in factors]
    for h in range(heads):
        cols = slice(h * HD, (h + 1) * HD)
        attended = 0.0
        for g in range(groups):
            attended += shares[g][:, h : h + 1] * parts[g, :, cols].astype(F32)
        attended = attended.astype(BF16)
        for g in range(out.shape[0]):
            out[g, :, cols] = attended


def cut_kernel(place, weight, *refs):
    outs, (held, arrived, left) = refs[:-3], refs[-3:]
    rows = held.shape[1]
    copies = []
    for i, out in enumerate(outs):
        k, start = i // PIECES, sum(o.shape[0] for o in outs[i // PIECES * PIECES : i])
        page = held.at[k, slice(start, start + out.shape[0]), :]
        part = pl.ds(pl.multiple_of(lax.rem(place[0] + k, 4) * rows + start, 16), out.shape[0])
        copies.append(
            (
                pltpu.make_async_copy(weight.at[part, :], page, arrived.at[i]),
                pltpu.make_async_copy(page, out, left.at[i]),
            )
        )
        copies[i][0].start()
    for arrival, departure in copies:
        arrival.wait()
        departure.start()
    for _, departure in copies:
        departure.wait()


def project_kernel(place, attended, *refs):
    weights, out = refs[:-1], refs[-1]
    size = out.shape[2]
    picked = [pl.ds(pl.multiple_of((2 * r + place[1]) * size, size), size) for r in range(out.shape[1])]
    rows = jnp.concatenate([attended[p, :] for p in picked], axis=0)
    for k in range(4):
        target = lax.rem(place[0] + 4 - k, 4)
        weight = jnp.concatenate([w[...] for w in weights[k * PIECES : (k + 1) * PIECES]], axis=0)
        term = jnp.dot(rows, weight, preferred_element_type=F32).astype(BF16)
        for r in range(out.shape[1]):
            out[target, r] = term[r * size : (r + 1) * size]


def swap(x, axes):
    return lax.all_to_all(x, axes, split_axis=0, concat_axis=0, tiled=False)


def along_y(x, distance):
    return lax.ppermute(x, "y", [(i, (i + distance) % 4) for i in range(4)])


def to_other(x, axis):
    return lax.ppermute(x, axis, [(0, 1), (1, 0)])


def shards(
    queries,
    new_keys,
    new_values,
    cache_keys,
    cache_values,
    span_ids,
    valid_len,
    pos_ids,
    offset,
    out_weight,
):
    y, core = lax.axis_index("y"), lax.axis_index("core")
    group = lax.axis_index("z") * 2 + lax.axis_index("x_hi")
    place = y[None].astype(jnp.int32)
    groups = 8
    fresh, width = queries.shape
    slots = span_ids.shape[0]
    rows = slots * SPAN
    quarter = width // 4
    tokens = pos_ids.shape[0]

    packet = jax.ShapeDtypeStruct((2, rows + fresh + 16, HD), BF16)
    with jax.named_scope("pack"):
        packets = pl.pallas_call(
            pack_kernel,
            out_shape=[packet] * 4,
            in_specs=[SMEM] * 4 + [ANY] * 4,
            out_specs=[VMEM] * 4,
            scratch_shapes=[
                pltpu.VMEM(cache_keys.shape, BF16),
                pltpu.VMEM(cache_keys.shape, BF16),
                pltpu.VMEM(new_keys.shape, BF16),
                pltpu.VMEM(new_keys.shape, BF16),
                pltpu.VMEM((2,) + packet.shape, BF16),
                pltpu.SemaphoreType.DMA((4,)),
            ],
            compiler_params=grant(56),
            cost_estimate=TINY,
        )(place, valid_len, span_ids, offset, cache_keys, cache_values, new_keys, new_values)
    with jax.named_scope("move_queries"):
        mine = swap(queries.reshape(fresh, 4, quarter).transpose(1, 0, 2), "y")
        mine, packets = lax.optimization_barrier((mine, packets))
        mine = mine.reshape(4 * fresh, quarter)
        mine = swap(jnp.broadcast_to(mine[None], (groups,) + mine.shape), ("z", "x_hi")).reshape(tokens, quarter)
    with jax.named_scope("move_kv"):
        kv = [packets[0]] + [along_y(packets[k], k) for k in range(1, 4)]
        all_live = jnp.stack([packet[0, rows + fresh, :slots] for packet in kv]).astype(jnp.int32).reshape(-1)

    columns = out_weight.shape[1]
    with jax.named_scope("move_weight"):
        sizes = (448, 288, 288)
        chunks = pl.pallas_call(
            cut_kernel,
            out_shape=[jax.ShapeDtypeStruct((size, columns), BF16) for size in sizes * 4],
            in_specs=[SMEM, ANY],
            out_specs=[ANY] * (4 * PIECES),
            scratch_shapes=[
                pltpu.VMEM((4, quarter, columns), BF16),
                pltpu.SemaphoreType.DMA((4 * PIECES,)),
                pltpu.SemaphoreType.DMA((4 * PIECES,)),
            ],
            compiler_params=grant(40),
            cost_estimate=TINY,
        )(place, lax.optimization_barrier((out_weight, packets))[0])

        def pieces(j, after):
            ready, _ = lax.optimization_barrier(([chunks[k * PIECES + j] for k in range(4)], after))
            return [ready[0]] + [along_y(ready[k], k) for k in range(1, 4)]

        weights = [pieces(j, kv[1:3]) for j in range(PIECES)]
        mine, chunks = lax.optimization_barrier((mine, chunks))

    pos_ids, chunks = lax.optimization_barrier((pos_ids, chunks))
    pos_n = [
        lax.dynamic_slice_in_dim(pos_ids, (group * 4 + lax.rem(y + 4 - k, 4)) * fresh, fresh) for k in range(4)
    ]
    pos_n = jnp.concatenate(pos_n + [jnp.full((KEY_BLOCK - 4 * fresh,), -1, jnp.int32)])[None]
    pos_q = pos_ids[:, None]

    capacity = 4 * (rows + fresh) + KEY_BLOCK
    heads = quarter // HD
    with jax.named_scope("attend"):
        partial = pl.pallas_call(
            attend_kernel,
            out_shape=jax.ShapeDtypeStruct((tokens, quarter + HD), BF16),
            in_specs=[SMEM] + [VMEM] * 7,
            out_specs=VMEM,
            scratch_shapes=[
                pltpu.VMEM((capacity, HD), BF16),
                pltpu.VMEM((capacity, 2 * HD), BF16),
                pltpu.VMEM((heads, tokens, HD), F32),
                pltpu.VMEM((heads, tokens, 2 * HD), F32),
            ],
            compiler_params=grant(22),
            cost_estimate=TINY,
        )(all_live, mine, *kv, pos_q, pos_n)

    with jax.named_scope("move_partials"):
        partial, weights[0] = lax.optimization_barrier((partial, weights[0]))
        partial = swap(partial.reshape(groups, tokens // groups, quarter + HD), ("z", "x_hi"))
    with jax.named_scope("settle"):
        attended = pl.pallas_call(
            settle_kernel,
            out_shape=jax.ShapeDtypeStruct((groups, tokens // groups, quarter), BF16),
            in_specs=[VMEM],
            out_specs=VMEM,
            compiler_params=grant(24),
            cost_estimate=TINY,
        )(partial)
    with jax.named_scope("move_attended"):
        attended, weights[1] = lax.optimization_barrier((attended, weights[1]))
        attended = swap(attended, ("z", "x_hi")).reshape(tokens, quarter)


    def project(which):
        return pl.pallas_call(
            project_kernel,
            out_shape=jax.ShapeDtypeStruct((4, 2, tokens // 4, columns), BF16),
            in_specs=[SMEM] + [VMEM] * (1 + 4 * PIECES),
            out_specs=VMEM,
            compiler_params=grant(32),
            cost_estimate=TINY,
        )(jnp.stack([y, which]).astype(jnp.int32), attended, *[w[k] for k in range(4) for w in weights])

    with jax.named_scope("project"):
        theirs = to_other(project(1 - core), "core")
        terms = (project(core).astype(F32) + theirs.astype(F32)).astype(BF16)
    with jax.named_scope("move_terms"):
        terms = swap(terms.reshape(8, tokens // 4, columns), ("y", "x_lo"))
    return jnp.sum(terms.astype(F32), axis=0).astype(BF16)


def solution(mesh):
    fine = Mesh(mesh.devices.reshape(4, 2, 4, 2, 2), ("z", "x_hi", "y", "x_lo", "core"))
    ctx, head = ("z", "x_hi", "y"), ("x_lo", "core")
    in_specs = (
        P(ctx, head),
        P(ctx, head),
        P(ctx, head),
        P(ctx, head),
        P(ctx, head),
        P(ctx),
        P(ctx),
        P(),
        P(),
        P(head, ctx),
    )
    return jax.shard_map(shards, mesh=fine, in_specs=in_specs, out_specs=P(head, ctx), check_vma=False)
```

```python
import functools
import math

import jax
import jax.numpy as jnp
import numpy as np
from jax import lax
from jax.experimental import pallas as pl
from jax.experimental.pallas import tpu as pltpu
from jax.sharding import Mesh
from jax.sharding import PartitionSpec as P

HD = 128
SPAN = 128
KEY_BLOCK = 512
FILL = -1e30
LOWEST = -1e20
LOG2_SCALE = math.log2(math.e) / math.sqrt(HD)
F32 = jnp.float32
BF16 = jnp.bfloat16
TINY = pl.CostEstimate(flops=1, bytes_accessed=1, transcendentals=0)
VMEM = pl.BlockSpec(memory_space=pltpu.VMEM)
SMEM = pl.BlockSpec(memory_space=pltpu.SMEM)
ANY = pl.BlockSpec(memory_space=pl.ANY)


def dot_nt(a, b):
    return lax.dot_general(a, b, (((1,), (1,)), ((), ())), preferred_element_type=F32)


def grant(mib):
    return pltpu.CompilerParams(vmem_limit_bytes=mib << 20)


def pack_kernel(place, valid_len, span_ids, offset, keys_in, values_in, new_keys_in, new_values_in, *refs):
    outs, (keys, values, new_keys, new_values, heads, sems) = refs[:4], refs[4:]
    copies = [
        pltpu.make_async_copy(source, target, sems.at[i])
        for i, (source, target) in enumerate(
            ((keys_in, keys), (values_in, values), (new_keys_in, new_keys), (new_values_in, new_values))
        )
    ]
    for copy in copies:
        copy.start()
    slots = valid_len.shape[0]
    rows = slots * SPAN
    fresh = new_keys.shape[0]
    row_id = lax.broadcasted_iota(jnp.int32, (SPAN, HD), 0)
    lane_id = lax.broadcasted_iota(jnp.int32, (16, HD), 1)
    live = [
        jnp.clip(jnp.minimum(valid_len[s], offset[0] - span_ids[s] * SPAN), 0, SPAN) for s in range(slots)
    ]
    counts = jnp.zeros((16, HD), F32)
    for s in range(slots):
        counts = jnp.where(lane_id == s, live[s].astype(F32), counts)
    for copy in copies:
        copy.wait()
    for head in range(2):
        cols = slice(head * HD, (head + 1) * HD)
        for s in range(slots):
            part = slice(s * SPAN, (s + 1) * SPAN)
            visible = row_id < live[s]
            key = keys[part, cols].astype(F32)
            key = jnp.where(visible, key, jnp.broadcast_to(key[:1], key.shape))
            heads[head, 0, part, :] = key.astype(BF16)
            heads[head, 1, part, :] = jnp.where(visible, values[part, cols].astype(F32), 0.0).astype(BF16)
        heads[head, 0, rows : rows + fresh, :] = new_keys[:, cols]
        heads[head, 1, rows : rows + fresh, :] = new_values[:, cols]
        heads[head, 0, rows + fresh :, :] = counts.astype(BF16)
        heads[head, 1, rows + fresh :, :] = counts.astype(BF16)
    for k, out in enumerate(outs):
        out[...] = heads[lax.rem(place[0] + k, 4) // 2]


def attend_kernel(live, queries, kv0, kv1, kv2, kv3, pos_q, pos_n, out, kc, vc, top, acc):
    sources = (kv0, kv1, kv2, kv3)
    slots = live.shape[0] // len(sources)
    rows = slots * SPAN
    fresh = kv0.shape[1] - rows - 16
    heads = queries.shape[1] // HD
    tokens = queries.shape[0]
    row_id = lax.broadcasted_iota(jnp.int32, (SPAN, HD), 0)
    start = len(sources) * fresh

    def rounded(count):
        return ((count + 15) // 16) * 16

    place = jnp.int32(start)
    for i, kv in enumerate(sources):
        target = slice(i * fresh, (i + 1) * fresh)
        kc[target, :] = kv[0, rows : rows + fresh, :]
        vc[target, :HD] = kv[1, rows : rows + fresh, :]
        vc[target, HD:] = jnp.ones((fresh, HD), BF16)

        def gather_slot(s, at, kv=kv, i=i):
            count = live[i * slots + s]
            source = pl.ds(pl.multiple_of(s * SPAN, SPAN), SPAN)
            target = pl.ds(pl.multiple_of(at, 16), SPAN)
            kc[target, :] = kv[0, source, :]
            vc[target, :HD] = kv[1, source, :]
            vc[target, HD:] = jnp.where(row_id < count, 1.0, 0.0).astype(BF16)
            return at + rounded(count)

        place = lax.fori_loop(0, slots, gather_slot, place)
    tail = pl.ds(pl.multiple_of(place, 16), KEY_BLOCK)
    spare = kc[start : start + 16, :].astype(F32)[:1]
    spare = jnp.where(place > start, spare, 0.0)
    kc[tail, :] = jnp.broadcast_to(spare, (KEY_BLOCK, HD)).astype(BF16)
    vc[tail, :] = jnp.zeros((KEY_BLOCK, 2 * HD), BF16)
    blocks = (place + KEY_BLOCK - 1) // KEY_BLOCK

    lane_id = lax.broadcasted_iota(jnp.int32, (tokens, HD), 1)
    key_id = lax.broadcasted_iota(jnp.int32, (1, KEY_BLOCK), 1)
    seen = jnp.where(key_id < place, pos_n[...], tokens) <= pos_q[...]
    lanes = [slice(j * HD, (j + 1) * HD) for j in range(KEY_BLOCK // HD)]

    def head_cols(h):
        return slice(h * HD, (h + 1) * HD)

    def rounded_max(s):
        high = functools.reduce(jnp.maximum, [s[:, g] for g in lanes])
        m = jnp.maximum(jnp.max(high, axis=1, keepdims=True) * LOG2_SCALE, LOWEST)
        return jnp.broadcast_to(m.astype(BF16).astype(F32), (tokens, HD))

    def score(h, part):
        return dot_nt(queries[:, head_cols(h)], kc[part, :])

    def sums(s, m, part):
        p = jnp.concatenate([jnp.exp2(s[:, g] * LOG2_SCALE - m).astype(BF16) for g in lanes], axis=1)
        return jnp.dot(p, vc[part, :], preferred_element_type=F32)

    def begin(h, part, s):
        s = jnp.where(seen, s, FILL)
        m = rounded_max(s)
        top[h] = m
        acc[h] = sums(s, m, part)

    def add(h, part, s):
        old = top[h]
        m = jnp.maximum(old, rounded_max(s))
        top[h] = m
        shrink = jnp.exp2(old - m)
        term = sums(s, m, part)
        acc[h, :, :HD] = acc[h, :, :HD] * shrink + term[:, :HD]
        acc[h, :, HD:] = acc[h, :, HD:] * shrink + term[:, HD:]

    def every_head(visit, part):
        s = score(0, part)
        for h in range(heads):
            following = score(h + 1, part) if h + 1 < heads else None
            visit(h, part, s)
            s = following

    every_head(begin, slice(0, KEY_BLOCK))

    def step(b, _):
        every_head(add, pl.ds(pl.multiple_of(b * KEY_BLOCK, KEY_BLOCK), KEY_BLOCK))
        return _

    lax.fori_loop(1, blocks, step, 0)

    notes = jnp.zeros((tokens, HD), F32)
    for h in range(heads):
        total = acc[h, :, HD:]
        high = total.astype(BF16).astype(F32)
        out[:, head_cols(h)] = acc[h, :, :HD].astype(BF16)
        notes = jnp.where(lane_id == h, top[h], notes)
        notes = jnp.where(lane_id == heads + h, high, notes)
        notes = jnp.where(lane_id == 2 * heads + h, total - high, notes)
    out[:, heads * HD :] = notes.astype(BF16)


def settle_kernel(parts, out):
    groups, tokens, width = parts.shape
    heads = width // HD - 1
    lane_id = lax.broadcasted_iota(jnp.int32, (tokens, HD), 1)
    notes = [parts[g, :, heads * HD :].astype(F32) for g in range(groups)]
    highest = functools.reduce(jnp.maximum, notes)
    factors = [jnp.exp2(jnp.where(lane_id < heads, n - highest, 0.0)) for n in notes]
    total = 0.0
    for factor, n in zip(factors, notes):
        total += factor * (pltpu.roll(n, HD - heads, 1) + pltpu.roll(n, HD - 2 * heads, 1))
    shares = [factor / jnp.where(lane_id < heads, total, 1.0) for factor in factors]
    for h in range(heads):
        cols = slice(h * HD, (h + 1) * HD)
        attended = 0.0
        for g in range(groups):
            attended += shares[g][:, h : h + 1] * parts[g, :, cols].astype(F32)
        attended = attended.astype(BF16)
        for g in range(out.shape[0]):
            out[g, :, cols] = attended


def cut_kernel(place, weight, *refs):
    outs, (held, arrived, left) = refs[:-3], refs[-3:]
    rows = held.shape[1]
    copies = []
    for i, (k, start) in enumerate(((0, 0), (1, 0), (3, 0), (2, 0), (2, rows // 2))):
        size = outs[i].shape[0]
        page = held.at[k, slice(start, start + size), :]
        part = pl.ds(pl.multiple_of(lax.rem(place[0] + k, 4) * rows + start, 16), size)
        copies.append(
            (
                pltpu.make_async_copy(weight.at[part, :], page, arrived.at[i]),
                pltpu.make_async_copy(page, outs[i], left.at[i]),
            )
        )
        copies[i][0].start()
    for arrival, departure in copies:
        arrival.wait()
        departure.start()
    for _, departure in copies:
        departure.wait()


def project_kernel(place, attended, w0, w1, w2a, w2b, w3, out):
    size = out.shape[2]
    picked = [pl.ds(pl.multiple_of((2 * r + place[1]) * size, size), size) for r in range(out.shape[1])]
    rows = jnp.concatenate([attended[p, :] for p in picked], axis=0)
    for k, pieces in enumerate(((w0,), (w1,), (w2a, w2b), (w3,))):
        target = lax.rem(place[0] + 4 - k, 4)
        weight = jnp.concatenate([w[...] for w in pieces], axis=0)
        term = jnp.dot(rows, weight, preferred_element_type=F32).astype(BF16)
        for r in range(out.shape[1]):
            out[target, r] = term[r * size : (r + 1) * size]


def swap(x, axes):
    return lax.all_to_all(x, axes, split_axis=0, concat_axis=0, tiled=False)


def along_y(x, distance):
    return lax.ppermute(x, "y", [(i, (i + distance) % 4) for i in range(4)])


def to_other(x, axis):
    return lax.ppermute(x, axis, [(0, 1), (1, 0)])


def shards(
    queries,
    new_keys,
    new_values,
    cache_keys,
    cache_values,
    span_ids,
    valid_len,
    pos_ids,
    offset,
    out_weight,
):
    y, core = lax.axis_index("y"), lax.axis_index("core")
    group = lax.axis_index("z") * 2 + lax.axis_index("x_hi")
    place = y[None].astype(jnp.int32)
    groups = 8
    fresh, width = queries.shape
    slots = span_ids.shape[0]
    rows = slots * SPAN
    quarter = width // 4
    tokens = pos_ids.shape[0]

    packet = jax.ShapeDtypeStruct((2, rows + fresh + 16, HD), BF16)
    with jax.named_scope("pack"):
        packets = pl.pallas_call(
            pack_kernel,
            out_shape=[packet] * 4,
            in_specs=[SMEM] * 4 + [ANY] * 4,
            out_specs=[VMEM] * 4,
            scratch_shapes=[
                pltpu.VMEM(cache_keys.shape, BF16),
                pltpu.VMEM(cache_keys.shape, BF16),
                pltpu.VMEM(new_keys.shape, BF16),
                pltpu.VMEM(new_keys.shape, BF16),
                pltpu.VMEM((2,) + packet.shape, BF16),
                pltpu.SemaphoreType.DMA((4,)),
            ],
            compiler_params=grant(56),
            cost_estimate=TINY,
        )(place, valid_len, span_ids, offset, cache_keys, cache_values, new_keys, new_values)
    with jax.named_scope("move_queries"):
        mine = swap(queries.reshape(fresh, 4, quarter).transpose(1, 0, 2), "y")
        mine, packets = lax.optimization_barrier((mine, packets))
        mine = mine.reshape(4 * fresh, quarter)
        mine = swap(jnp.broadcast_to(mine[None], (groups,) + mine.shape), ("z", "x_hi")).reshape(tokens, quarter)
    with jax.named_scope("move_kv"):
        kv = [packets[0]] + [along_y(packets[k], k) for k in range(1, 4)]
        all_live = jnp.stack([packet[0, rows + fresh, :slots] for packet in kv]).astype(jnp.int32).reshape(-1)

    columns = out_weight.shape[1]
    with jax.named_scope("move_weight"):
        sizes = (quarter, quarter, quarter, quarter // 2, quarter // 2)
        chunks = pl.pallas_call(
            cut_kernel,
            out_shape=[jax.ShapeDtypeStruct((size, columns), BF16) for size in sizes],
            in_specs=[SMEM, ANY],
            out_specs=[ANY] * len(sizes),
            scratch_shapes=[
                pltpu.VMEM((4, quarter, columns), BF16),
                pltpu.SemaphoreType.DMA((len(sizes),)),
                pltpu.SemaphoreType.DMA((len(sizes),)),
            ],
            compiler_params=grant(40),
            cost_estimate=TINY,
        )(place, lax.optimization_barrier((out_weight, packets))[0])
        moving, _ = lax.optimization_barrier((chunks[1:], kv[1:3]))
        around = [along_y(moving[0], 1), along_y(moving[1], 3)]
        across = [along_y(moving[2], 2), along_y(moving[3], 2)]
        mine, chunks = lax.optimization_barrier((mine, chunks))

    pos_ids, chunks = lax.optimization_barrier((pos_ids, chunks))
    pos_n = [
        lax.dynamic_slice_in_dim(pos_ids, (group * 4 + lax.rem(y + 4 - k, 4)) * fresh, fresh) for k in range(4)
    ]
    pos_n = jnp.concatenate(pos_n + [jnp.full((KEY_BLOCK - 4 * fresh,), -1, jnp.int32)])[None]
    pos_q = pos_ids[:, None]

    capacity = 4 * (rows + fresh) + KEY_BLOCK
    heads = quarter // HD
    with jax.named_scope("attend"):
        partial = pl.pallas_call(
            attend_kernel,
            out_shape=jax.ShapeDtypeStruct((tokens, quarter + HD), BF16),
            in_specs=[SMEM] + [VMEM] * 7,
            out_specs=VMEM,
            scratch_shapes=[
                pltpu.VMEM((capacity, HD), BF16),
                pltpu.VMEM((capacity, 2 * HD), BF16),
                pltpu.VMEM((heads, tokens, HD), F32),
                pltpu.VMEM((heads, tokens, 2 * HD), F32),
            ],
            compiler_params=grant(22),
            cost_estimate=TINY,
        )(all_live, mine, *kv, pos_q, pos_n)

    with jax.named_scope("move_partials"):
        partial, around = lax.optimization_barrier((partial, around))
        partial = swap(partial.reshape(groups, tokens // groups, quarter + HD), ("z", "x_hi"))
    with jax.named_scope("settle"):
        attended = pl.pallas_call(
            settle_kernel,
            out_shape=jax.ShapeDtypeStruct((groups, tokens // groups, quarter), BF16),
            in_specs=[VMEM],
            out_specs=VMEM,
            compiler_params=grant(10),
            cost_estimate=TINY,
        )(partial)
    with jax.named_scope("move_attended"):
        attended, across[0] = lax.optimization_barrier((attended, across[0]))
        attended = swap(attended, ("z", "x_hi")).reshape(tokens, quarter)


    def project(which):
        return pl.pallas_call(
            project_kernel,
            out_shape=jax.ShapeDtypeStruct((4, 2, tokens // 4, columns), BF16),
            in_specs=[SMEM] + [VMEM] * 6,
            out_specs=VMEM,
            compiler_params=grant(14),
            cost_estimate=TINY,
        )(jnp.stack([y, which]).astype(jnp.int32), attended, chunks[0], around[0], *across, around[1])

    with jax.named_scope("project"):
        theirs = to_other(project(1 - core), "core")
        terms = (project(core).astype(F32) + theirs.astype(F32)).astype(BF16)
    with jax.named_scope("move_terms"):
        terms = swap(terms.reshape(8, tokens // 4, columns), ("y", "x_lo"))
    return jnp.sum(terms.astype(F32), axis=0).astype(BF16)


def solution(mesh):
    fine = Mesh(mesh.devices.reshape(4, 2, 4, 2, 2), ("z", "x_hi", "y", "x_lo", "core"))
    ctx, head = ("z", "x_hi", "y"), ("x_lo", "core")
    in_specs = (
        P(ctx, head),
        P(ctx, head),
        P(ctx, head),
        P(ctx, head),
        P(ctx, head),
        P(ctx),
        P(ctx),
        P(),
        P(),
        P(head, ctx),
    )
    return jax.shard_map(shards, mesh=fine, in_specs=in_specs, out_specs=P(head, ctx), check_vma=False)
```
